256 devices in a mesh: space: 64 (over y_hi, z, x), chan: 4 (over y_lo, core).
Axes of the slice: x: 4, y: 4 (y_hi: 2, y_lo: 2; y = y_hi * 2 + y_lo), z: 8, core: 2. Of those that a mesh axis runs over, the one named last changes fastest.
Arguments:
- grid_state: bfloat16 [192, 720, 512], P('space'), may hold values from -6 to 6
- fold_columns: int32 [720], replicated, may hold values from 0 to 719, each once
- mesh_state: bfloat16 [10240, 512], P('space', 'chan'), may hold values from -6 to 6
- edge_state: bfloat16 [327680, 512], P('space'), may hold values from -6 to 6
- conv_weight: bfloat16 [3, 3, 512, 512], P(None, None, None, 'chan'), may hold values from -0.09375 to 0.09375
- conv_bias: bfloat16 [512], P('chan'), may hold values from -3 to 3
- source_weight: bfloat16 [512, 512], P(None, 'chan'), may hold values from -0.25 to 0.25
- target_weight: bfloat16 [512, 512], P(None, 'chan'), may hold values from -0.25 to 0.25
- edge_weight: bfloat16 [512, 512], P(None, 'chan'), may hold values from -0.25 to 0.25
- edge_bias: bfloat16 [512], P('chan'), may hold values from -3 to 3
- message_weight: bfloat16 [512, 512], replicated, may hold values from -0.25 to 0.25
- self_weight: bfloat16 [512, 512], P(None, 'chan'), may hold values from -0.1875 to 0.1875
- inbox_weight: bfloat16 [512, 512], P(None, 'chan'), may hold values from -0.1875 to 0.1875
- node_bias: bfloat16 [512], P('chan'), may hold values from -3 to 3
- output_weight: bfloat16 [512, 512], replicated
- output_gain: float32 [512], replicated, may hold values from 0.1 to 1.9
- cell_node: int32 [192, 720], P('space'), may hold values from 0 to 159
- cell_weight: float32 [192, 720], P('space'), may hold values from 0.2 to 1
- edge_source: int32 [327680], P('space'), may hold values from 0 to 2207, as said below
- edge_target: int32 [327680], P('space'), may hold values from 0 to 159
- edge_count: int32 [64], P('space'), may hold values from 1024 to 5120, as said below
- send_rows: int32 [64, 64, 32], P('space'), may hold values from 0 to 159
- read_node: int32 [3, 192, 720], P(None, 'space'), may hold values from 0 to 159
- read_weight: float32 [3, 192, 720], P(None, 'space'), may hold values from 0.2 to 1
Outputs:
- node_out: bfloat16 [10240, 512], P('space', 'chan')
- grid_out: bfloat16 [192, 720, 512], P('space', None, 'chan')
The draws below stay inside these ranges and needn't reach their ends.
Inputs may be any that keep to these rules, and one draw needn't show every extreme that they name: fold_columns is a permutation of the 720 columns. send_rows[q, p, k] is a node of partition q, by its index within q, sent to partition p in slot k. `edge_source`: a value below 160 names a node of the edge's own partition; a larger value names slot (s - 160) % 32 of the rows sent by partition (s - 160) // 32. The live edges of a partition are its first edge_count slots; some partition has 5120 live edges in every draw.
All inputs are finite; a program needn't handle non-finite values.
Results may differ from the reference program's by a relative error of at most 0.0095.
Values may be sent and summed in bfloat16 or wider, within the bound.
A program may use at most 64 MiB of HBM per device.

```python
import math
import jax
import jax.numpy as jnp
from jax import lax

D = 512
GR = 3
LON = 720
M_DEV = 160
E_DEV = 5120
CAP = 32
PEERS = 64
ROWS = 192
NODES = 10240
EDGES = 327680


def draw_edge_source(key, part):
    key = jax.random.fold_in(key, 11)
    pick_key, local_key, remote_key = jax.random.split(key, 3)
    choose_local = jax.random.randint(pick_key, (EDGES,), 0, 2)
    local_ids = jax.random.randint(local_key, (EDGES,), 0, M_DEV)
    remote_ids = jax.random.randint(remote_key, (EDGES,), M_DEV, M_DEV + PEERS * CAP)
    return jnp.where(choose_local == 1, local_ids, remote_ids).astype(jnp.int32)


def draw_edge_count(key, part):
    key = jax.random.fold_in(key, 12)
    level_key, place_key = jax.random.split(key)
    levels = jax.random.randint(level_key, (PEERS,), 1, 6)
    counts = E_DEV // levels
    busiest = jax.random.randint(place_key, (), 0, PEERS)
    device_ids = jnp.arange(PEERS)
    counts = jnp.where(device_ids == busiest, E_DEV, counts)
    counts = jnp.where(device_ids == (busiest + 1) % PEERS, E_DEV // 5, counts)
    return counts.astype(jnp.int32)


def draw_output_weight(key, part):
    key = jax.random.fold_in(key, 13)
    entry_key, scale_key = jax.random.split(key, 2)
    column_scale = jnp.exp(jax.random.uniform(scale_key, (1, D), jnp.float32, math.log(0.3), math.log(3.0)))
    entries = jax.random.normal(entry_key, (D, D), jnp.float32)
    return (entries * column_scale * D ** (-0.5)).astype(jnp.bfloat16)


def set_ends(values, own_key, smallest, top_value):
    shape = values.shape
    place = [jax.random.randint(jax.random.fold_in(own_key, axis), (), 0, shape[axis]) for axis in range(len(shape))]
    values = values.at[tuple(place)].set(smallest)
    longest = shape.index(max(shape))
    place[longest] = (place[longest] + 1) % shape[longest]
    return values.at[tuple(place)].set(top_value)


def steps_of(own_key, extent, pieces, least, high):
    loudness = 1.0
    for dim, parts in pieces:
        draws = jax.random.uniform(jax.random.fold_in(jax.random.fold_in(own_key, 6), dim), (parts,), jnp.float32, least / len(pieces), high / len(pieces))
        loudness = loudness * jnp.repeat(jnp.exp(draws), extent[dim] // parts).reshape((-1,) + (1,) * (len(extent) - 1 - dim))
    return loudness


def gaussian(key, dims, scale, limit, shards=(), kind=jnp.bfloat16):
    loudness = steps_of(key, dims, shards, -0.22, 0.18) if shards else 1.0
    drawn = jax.random.normal(key, dims, jnp.float32) * scale * loudness
    return jnp.minimum(jnp.maximum(drawn, -limit), limit).astype(kind)


def setup_inputs(seed: int = 0) -> dict:
    seeds = jax.random.split(jax.random.key(seed), 25)
    return {
        "grid_state": gaussian(seeds[0], (ROWS, LON, D), 1.0, 6.0, ((0, 64),)),
        "fold_columns": jax.random.permutation(seeds[1], LON).astype(jnp.int32),
        "mesh_state": gaussian(seeds[2], (NODES, D), 1.0, 6.0, ((0, 64), (1, 4))),
        "edge_state": gaussian(seeds[3], (EDGES, D), 1.0, 6.0, ((0, 64),)),
        "conv_weight": gaussian(seeds[4], (3, 3, D, D), (9 * D) ** -0.5, 0.09375, ((3, 4),)),
        "conv_bias": gaussian(seeds[5], (D,), 0.5, 3.0, ((0, 4),)),
        "source_weight": gaussian(seeds[6], (D, D), D ** -0.5, 0.25, ((1, 4),)),
        "target_weight": gaussian(seeds[7], (D, D), D ** -0.5, 0.25, ((1, 4),)),
        "edge_weight": gaussian(seeds[8], (D, D), D ** -0.5, 0.25, ((1, 4),)),
        "edge_bias": gaussian(seeds[9], (D,), 0.5, 3.0, ((0, 4),)),
        "message_weight": gaussian(seeds[10], (D, D), D ** -0.5, 0.25),
        "self_weight": gaussian(seeds[11], (D, D), (2 * D) ** -0.5, 0.1875, ((1, 4),)),
        "inbox_weight": gaussian(seeds[12], (D, D), (2 * D) ** -0.5, 0.1875, ((1, 4),)),
        "node_bias": gaussian(seeds[13], (D,), 0.5, 3.0, ((0, 4),)),
        "output_weight": draw_output_weight(jax.random.fold_in(seeds[24], 71), 0),
        "output_gain": jnp.clip(1.0 + 0.18 * jax.random.normal(seeds[15], (D,), jnp.float32), 0.1, 1.9),
        "cell_node": set_ends(jax.random.randint(seeds[16], (ROWS, LON), 0, M_DEV), jax.random.fold_in(seeds[16], 1), 0, M_DEV - 1).astype(jnp.int32),
        "cell_weight": jnp.clip(0.2 + 0.8 * jax.random.uniform(seeds[17], (ROWS, LON), jnp.float32) ** steps_of(seeds[17], (ROWS, LON), ((0, 64),), -0.2, 0.2), 0.2, 1.0),
        "edge_source": draw_edge_source(jax.random.fold_in(seeds[24], 71), 0),
        "edge_target": set_ends(jax.random.randint(seeds[19], (EDGES,), 0, M_DEV), jax.random.fold_in(seeds[19], 1), 0, M_DEV - 1).astype(jnp.int32),
        "edge_count": draw_edge_count(jax.random.fold_in(seeds[24], 71), 0),
        "send_rows": set_ends(jax.random.randint(seeds[21], (PEERS, PEERS, CAP), 0, M_DEV), jax.random.fold_in(seeds[21], 1), 0, M_DEV - 1).astype(jnp.int32),
        "read_node": set_ends(jax.random.randint(seeds[22], (3, ROWS, LON), 0, M_DEV), jax.random.fold_in(seeds[22], 1), 0, M_DEV - 1).astype(jnp.int32),
        "read_weight": jnp.clip(0.2 + 0.8 * jax.random.uniform(seeds[23], (3, ROWS, LON), jnp.float32) ** steps_of(seeds[23], (3, ROWS, LON), ((1, 64),), -0.2, 0.2), 0.2, 1.0),
    }


norm_eps = 1e-05

def pad_grid(grid_state, fold_columns):
    north_row = grid_state[-1][fold_columns]
    south_row = jnp.zeros_like(grid_state[0])
    tall_grid = jnp.concatenate([south_row[None], grid_state, north_row[None]], axis=0)
    return jnp.concatenate([tall_grid[:, -1:], tall_grid, tall_grid[:, :1]], axis=1)

def reference(grid_state, fold_columns, mesh_state, edge_state, conv_weight, conv_bias, source_weight, target_weight, edge_weight, edge_bias, message_weight, self_weight, inbox_weight, node_bias, output_weight, output_gain, cell_node, cell_weight, edge_source, edge_target, edge_count, send_rows, read_node, read_weight):
    padded = pad_grid(grid_state, fold_columns)
    features = grid_state.shape[2]
    summed = jnp.zeros((ROWS * LON, features), jnp.float32)
    for shift_row in range(3):
        for shift_col in range(3):
            window = padded[shift_row:shift_row + ROWS, shift_col:shift_col + LON, :].reshape(ROWS * LON, features)
            summed = summed + jnp.dot(window, conv_weight[shift_row, shift_col], preferred_element_type=jnp.float32)
    conv = summed + conv_bias.astype(jnp.float32)
    weighted = jax.nn.silu(conv) * cell_weight.reshape(-1)[:, None]
    band_of_row = (jnp.arange(ROWS, dtype=jnp.int32) // GR)[:, None]
    cell_ids = (band_of_row * M_DEV + cell_node).reshape(-1)
    agg = jax.ops.segment_sum(weighted, cell_ids, num_segments=NODES)
    nodes = (mesh_state.astype(jnp.float32) + agg).astype(jnp.bfloat16)
    sent = jnp.dot(nodes, source_weight, preferred_element_type=jnp.float32).astype(jnp.bfloat16)
    recv = jnp.dot(nodes, target_weight, preferred_element_type=jnp.float32)

    def partition_pool(partition):
        first_edge = (partition * E_DEV).astype(jnp.int32)
        feats = lax.dynamic_slice_in_dim(edge_state, first_edge, E_DEV, 0)
        sources = lax.dynamic_slice_in_dim(edge_source, first_edge, E_DEV, 0)
        targets = lax.dynamic_slice_in_dim(edge_target, first_edge, E_DEV, 0)
        remote = sources - M_DEV
        peer_ids = jnp.clip(remote // CAP, 0, PEERS - 1).astype(jnp.int32)
        slot_ids = (remote % CAP).astype(jnp.int32)
        remote_node = send_rows[peer_ids, partition, slot_ids]
        sender = jnp.where(sources < M_DEV, partition * M_DEV + sources, peer_ids * M_DEV + remote_node).astype(jnp.int32)
        local_recv = lax.dynamic_slice_in_dim(recv, (partition * M_DEV).astype(jnp.int32), M_DEV, 0)
        pre_act = sent[sender].astype(jnp.float32) + local_recv[targets]
        pre_act = pre_act + jnp.dot(feats, edge_weight, preferred_element_type=jnp.float32) + edge_bias.astype(jnp.float32)
        live_mask = (jnp.arange(E_DEV, dtype=jnp.int32) < edge_count[partition]).astype(jnp.bfloat16)
        edge_hidden = jax.nn.silu(pre_act).astype(jnp.bfloat16) * live_mask[:, None]
        return jax.ops.segment_sum(edge_hidden.astype(jnp.float32), targets, num_segments=M_DEV)
    pooled = lax.map(partition_pool, jnp.arange(PEERS, dtype=jnp.int32)).reshape(NODES, features).astype(jnp.bfloat16)
    message = jnp.dot(pooled, message_weight, preferred_element_type=jnp.float32).astype(jnp.bfloat16)
    node_pre = jnp.dot(nodes, self_weight, preferred_element_type=jnp.float32) + jnp.dot(message, inbox_weight, preferred_element_type=jnp.float32)
    node_hidden = jax.nn.silu(node_pre + node_bias.astype(jnp.float32)).astype(jnp.bfloat16)
    update = jnp.dot(node_hidden, output_weight, preferred_element_type=jnp.float32)
    row_mean = lax.optimization_barrier(jnp.mean(update, axis=1, keepdims=True))
    row_var = lax.optimization_barrier(jnp.mean(jnp.square(update - row_mean), axis=1, keepdims=True))
    normed = output_gain * (update - row_mean) * lax.rsqrt(row_var + norm_eps)
    node_out = (nodes.astype(jnp.float32) + normed).astype(jnp.bfloat16)
    read_ids = band_of_row[None] * M_DEV + read_node
    grid_sum = grid_state.astype(jnp.float32)
    for corner in range(3):
        grid_sum = grid_sum + read_weight[corner][..., None] * node_out[read_ids[corner]].astype(jnp.float32)
    grid_out = grid_sum.astype(jnp.bfloat16)
    return (node_out, grid_out)
```

```python
import jax
import jax.numpy as jnp
from jax import lax
from jax.experimental import pallas as pl
from jax.experimental.pallas import tpu as pltpu
from jax.sharding import PartitionSpec as P

f32 = jnp.float32
bf16 = jnp.bfloat16
i32 = jnp.int32
norm_eps = 1e-05
MESH = pl.DeviceIdType.MESH

SPACE, CHAN = 64, 4
NY, NZ, NX = 2, 8, 4
FEAT, COLS = 512, 128
BAND, LON = 3, 720
NODES = 160
EDGES = 5120
CAP = 32
MCH = 240
LONP = 768
SHIFTS = (4, 0, 3, 5, 2, 6, 1, 7)


def dot(a, b):
    return jnp.dot(a, b, preferred_element_type=f32)


def silu(v):
    return 0.5 * v * (1.0 + jnp.tanh(0.5 * v))


def kernel(
    grid_h, fold_h, mesh_h, edge_h, convw_h, convb_h, srcw_h, tgtw_h, edgew_h, edgeb_h,
    msgw_h, selfw_h, inw_h, nodeb_h, outw_h, gain_h, celln_h, cellw_h, esrc_h, etgt_h,
    ecount, send_h, readn_h, readw_h,
    node_out, grid_out,
    x, fold, mesh_v, edge, wcat, convb, srcw, tgtw, edgew, edgeb,
    msgw, selfw, inw, nodeb, outw, gain, celln, cellw, esrc, etgt, sendr, readn, readw,
    z, cpart, halo_out, halo_in, act, inc_a, sel_o, outg, table, nodes4, pool4, hid4,
    onehot, half_b, pool_p, acc1, acc2, incoming, ridx, rwt, rmat, upd, srcc,
    load_sem, halo_send, halo_recv, gat_send, gat_recv, a2a_send, a2a_recv,
):
    me = lax.axis_index("space")
    ch = lax.axis_index("chan")
    my, mz, mx = me // 32, (me // 4) % 8, me % 4

    loads = {}

    def load(name, src, dst):
        k = len(loads)
        c = pltpu.make_async_copy(src, dst, load_sem.at[k])
        c.start()
        loads[name] = c

    def ready(*names):
        for name in names:
            loads[name].wait()

    def load_w(a):
        for b in range(3):
            load(("w", a, b), convw_h.at[a, b], wcat.at[a, :, b * COLS:(b + 1) * COLS])

    load("x0", grid_h.at[0], x.at[0])
    load_w(2)
    load("x2", grid_h.at[2], x.at[2])
    load_w(0)
    load("x1", grid_h.at[1], x.at[1])
    load_w(1)
    for name, s, d in (
        ("convb", convb_h, convb), ("celln", celln_h, celln), ("cellw", cellw_h, cellw),
        ("sendr", send_h.at[0], sendr), ("esrc", esrc_h, esrc), ("etgt", etgt_h, etgt),
        ("fold", fold_h, fold), ("mesh", mesh_h, mesh_v), ("srcw", srcw_h, srcw), ("tgtw", tgtw_h, tgtw),
        ("edgew", edgew_h, edgew), ("edgeb", edgeb_h, edgeb),
        ("e0", edge_h.at[0:2560], edge.at[0:2560]), ("e1", edge_h.at[2560:5120], edge.at[2560:5120]),
        ("selfw", selfw_h, selfw), ("msgw", msgw_h, msgw), ("inw", inw_h, inw), ("nodeb", nodeb_h, nodeb),
        ("outw", outw_h, outw), ("gain", gain_h, gain), ("readn", readn_h, readn), ("readw", readw_h, readw),
    ):
        load(name, s, d)

    barrier = pltpu.get_barrier_semaphore()

    def greet(d, _):
        pl.semaphore_signal(barrier, inc=1, device_id={"space": (me + d) % SPACE}, device_id_type=MESH)
        return 0

    lax.fori_loop(1, SPACE, greet, 0)
    for d in range(1, CHAN):
        pl.semaphore_signal(barrier, inc=1, device_id={"chan": (ch + d) % CHAN}, device_id_type=MESH)

    def conv_z(terms):
        for m in range(LON // MCH):
            rows = pl.ds(m * MCH, MCH)
            acc = None
            for xr, a in terms:
                d = dot(xr[rows, :], wcat[a])
                acc = d if acc is None else acc + d
            z[pl.ds(8 + m * MCH, MCH), :] = acc
        z[7:8, 0:COLS] = z[LON + 7:LON + 8, 0:COLS]
        z[LON + 8:LON + 9, 2 * COLS:3 * COLS] = z[8:9, 2 * COLS:3 * COLS]

    def shifted(m):
        o = m * MCH
        return (
            z[pl.ds(o + 7, MCH), 0:COLS]
            + z[pl.ds(o + 8, MCH), COLS:2 * COLS]
            + z[pl.ds(o + 9, MCH), 2 * COLS:3 * COLS]
        )

    chunks = range(LON // MCH)

    ready("x0", ("w", 2, 0), ("w", 2, 1), ("w", 2, 2))
    conv_z([(x.at[0], 2)])
    for m in chunks:
        halo_out[0, pl.ds(m * MCH, MCH), :] = shifted(m).astype(bf16)
    pl.semaphore_wait(barrier, SPACE - 1 + CHAN - 1)

    def halo_copy(k):
        peer = (me + SPACE - 1) % SPACE if k == 0 else (me + 1) % SPACE
        return pltpu.make_async_remote_copy(
            src_ref=halo_out.at[k], dst_ref=halo_in.at[k], send_sem=halo_send.at[k], recv_sem=halo_recv.at[k],
            device_id={"space": peer}, device_id_type=MESH,
        )

    halo = [halo_copy(0), halo_copy(1)]
    halo[0].start()
    ready("x2", ("w", 0, 0), ("w", 0, 1), ("w", 0, 2))
    conv_z([(x.at[2], 0)])
    for m in chunks:
        halo_out[1, pl.ds(m * MCH, MCH), :] = shifted(m).astype(bf16)
    halo[1].start()

    ready("x1", ("w", 1, 0), ("w", 1, 1), ("w", 1, 2), "convb", "celln", "cellw")
    bias = convb[...].astype(f32)
    for r, terms in (
        (0, [(x.at[0], 1), (x.at[1], 2)]),
        (2, [(x.at[1], 0), (x.at[2], 1)]),
        (1, [(x.at[0], 0), (x.at[1], 1), (x.at[2], 2)]),
    ):
        conv_z(terms)
        for m in chunks:
            v = shifted(m) + bias
            rows = pl.ds(m * MCH, MCH)
            if r == 1:
                act[1, rows, :] = silu(v).astype(bf16)
            else:
                cpart[r // 2, rows, :] = v

    ready("fold")

    @pl.when(me == SPACE - 1)
    def _():
        def body(t, _):
            rows = pl.ds(pl.multiple_of(t * 16, 16), 16)
            ids = lax.broadcasted_iota(i32, (16, LON), 0) + t * 16
            pick = jnp.where(ids == fold[...], 1.0, 0.0).astype(bf16)
            srcc[rows, :] = pick
            return 0

        lax.fori_loop(0, LON // 16, body, 0)
        xf = lax.dot_general(srcc[...], x[2], (((0,), (0,)), ((), ())), preferred_element_type=f32)
        upd_x = xf.astype(bf16)
        onehot[0:LON, 0:FEAT] = upd_x
        conv_z([(onehot.at[0:LON, 0:FEAT], 2)])
        for m in chunks:
            rows = pl.ds(m * MCH, MCH)
            cpart[1, rows, :] = cpart[1, rows, :] + shifted(m)

    for r in range(BAND):
        ids = lax.broadcasted_iota(i32, (NODES, LON), 0)
        inc_a[r] = jnp.where(ids == celln[r:r + 1, :], cellw[r:r + 1, :], 0.0).astype(bf16)

    ready("sendr", "esrc", "etgt")
    send_t = sendr[...].astype(f32).T
    lane256 = lax.broadcasted_iota(i32, (CAP, 256), 1).astype(f32)
    for p in range(SPACE):
        sel_o[p * CAP:(p + 1) * CAP, :] = jnp.where(send_t[:, p:p + 1] == lane256, 1.0, 0.0).astype(bf16)

    s = esrc[...]
    u = s - NODES
    q = lax.shift_right_logical(u, 5) & 63
    k = u & 31
    dz = (mz - (lax.shift_right_logical(q, 2) & 7)) & 7
    dy = (my - lax.shift_right_logical(q, 5)) & 1
    dx = (mx - (q & 3)) & 3
    t = jnp.zeros_like(s)
    for pos, shift in enumerate(SHIFTS):
        t = jnp.where(dz == shift, pos, t)
    remote = 256 + lax.shift_right_logical(t, 1) * 256 + (dy * 4 + dx) * CAP + k
    col = jnp.where(u < 0, s, remote)
    halfbit = jnp.where(u < 0, 0, t & 1)
    slot = lax.broadcasted_iota(i32, s.shape, 0) * 128 + lax.broadcasted_iota(i32, s.shape, 1)
    live_t = jnp.where(slot < ecount[0], etgt[...], -1)
    srcc2 = col + 2048 * halfbit
    ridx[0] = srcc2
    ridx[1] = etgt[...]
    ridx[2] = live_t

    lane_f = lax.broadcasted_iota(i32, (128, 128), 1).astype(f32)

    def column(which, e):
        row = ridx[which, pl.ds(e, 1), :].astype(f32)
        return jnp.broadcast_to(row, (128, 128)).T

    def build(e, _):
        rows = pl.ds(pl.multiple_of(e * 128, 128), 128)
        c = column(0, e)
        hb = jnp.where(c >= 2048.0, 1.0, 0.0)
        half_b[rows, :] = hb.astype(bf16)
        c = c - 2048.0 * hb
        hi = jnp.floor(c * (1.0 / 128.0))
        lo = c - 128.0 * hi
        m = jnp.where(lo == lane_f, hi, -1.0).astype(bf16)
        one = jnp.ones((128, 128), bf16)
        zero = jnp.zeros((128, 128), bf16)
        for tile in range(10):
            at = tile if tile < 2 else tile + 2
            onehot[rows, at * 128:(at + 1) * 128] = jnp.where(m == jnp.asarray(tile, bf16), one, zero)
        c = column(1, e)
        for tile in range(2):
            onehot[rows, (2 + tile) * 128:(3 + tile) * 128] = jnp.where(
                c == lane_f + 128.0 * tile, 1.0, 0.0
            ).astype(bf16)
        ids = lax.broadcasted_iota(i32, (NODES, 128), 0)
        pool_p[:, rows] = jnp.where(ids == ridx[2, pl.ds(e, 1), :], 1.0, 0.0).astype(bf16)
        return 0

    FIRST = 20
    lax.fori_loop(0, FIRST, build, 0)

    halo[0].wait_recv()
    halo[1].wait_recv()
    south_ok = jnp.where(me > 0, 1.0, 0.0)
    north_ok = jnp.where(me < SPACE - 1, 1.0, 0.0)
    for m in chunks:
        rows = pl.ds(m * MCH, MCH)
        act[0, rows, :] = silu(cpart[0, rows, :] + halo_in[1, rows, :].astype(f32) * south_ok).astype(bf16)
        act[2, rows, :] = silu(cpart[1, rows, :] + halo_in[0, rows, :].astype(f32) * north_ok).astype(bf16)
    ready("mesh")
    agg = dot(inc_a[0], act[0]) + dot(inc_a[1], act[1]) + dot(inc_a[2], act[2])
    mine = (mesh_v[...].astype(f32) + agg).astype(bf16)

    def gather_start(buf, stage):
        out = []
        for d in range(1, CHAN):
            c = pltpu.make_async_remote_copy(
                src_ref=buf.at[ch], dst_ref=buf.at[ch],
                send_sem=gat_send.at[stage, d], recv_sem=gat_recv.at[stage, d],
                device_id={"chan": (ch + d) % CHAN}, device_id_type=MESH,
            )
            c.start()
            out.append(c)
        return out

    def gathered(buf):
        return jnp.concatenate([buf[0], buf[1], buf[2], buf[3]], axis=1)

    nodes4[ch] = mine
    g_nodes = gather_start(nodes4, 0)
    ready("srcw", "tgtw")
    lax.fori_loop(FIRST, FIRST + 4, build, 0)
    for c in g_nodes:
        c.wait_recv()
    nodes = gathered(nodes4)
    sent = dot(nodes, srcw[...]).astype(bf16)
    table[...] = jnp.zeros_like(table)
    table[0:NODES, :] = sent
    for b in range(SPACE * CAP // 256):
        picked = dot(sel_o[b * 256:(b + 1) * 256, :], table[0:256, :]).astype(bf16)
        outg[b * 8:(b + 1) * 8] = picked.reshape(8, CAP, COLS)

    def a2a_copy(pos, j):
        peer = ((my + j // 4) % NY) * 32 + ((mz + SHIFTS[pos]) % NZ) * 4 + (mx + j % 4) % NX
        sl = pos * 8 + j
        return pltpu.make_async_remote_copy(
            src_ref=outg.at[peer], dst_ref=incoming.at[sl], send_sem=a2a_send.at[sl], recv_sem=a2a_recv.at[sl],
            device_id={"space": peer}, device_id_type=MESH,
        )

    for pos in range(8):
        def go(j, _, pos=pos):
            a2a_copy(pos, j).start()
            return 0
        lax.fori_loop(1 if SHIFTS[pos] == 0 else 0, 8, go, 0)
    incoming[8] = outg[me]

    table[256:256 + NODES, :] = dot(nodes, tgtw[...]).astype(bf16)
    lax.fori_loop(FIRST + 4, EDGES // 128, build, 0)
    ready("edgew", "edgeb", "e0", "e1")
    ebias = edgeb[...].astype(f32)

    def own(e, _):
        rows = pl.ds(pl.multiple_of(e * 256, 256), 256)
        acc1[rows, :] = dot(edge[rows, :], edgew[...]) + dot(onehot[rows, 0:512], table[...]) + ebias
        return 0

    lax.fori_loop(0, EDGES // 256, own, 0)

    ready("selfw", "nodeb", "readn", "readw", "msgw", "inw", "outw", "gain")
    self_part = dot(nodes, selfw[...]) + nodeb[...].astype(f32)
    ids = lax.broadcasted_iota(i32, (NODES, LON), 0)
    for r in range(BAND):
        w = jnp.zeros((NODES, LON), f32)
        for corner in range(3):
            w = w + jnp.where(ids == readn[corner, r:r + 1, :], readw[corner, r:r + 1, :], 0.0)
        rwt[:, 0:LON] = w
        rwt[:, LON:LONP] = jnp.zeros((NODES, LONP - LON), f32)
        for tile in range(LONP // 128):
            rmat[r, tile * 128:(tile + 1) * 128, :] = rwt[:, tile * 128:(tile + 1) * 128].T.astype(bf16)

    def group_table(g):
        left = incoming[16 * g:16 * g + 8].reshape(256, COLS)
        right = incoming[16 * g + 8:16 * g + 16].reshape(256, COLS)
        return jnp.concatenate([left, right], axis=1)

    def arrive(g):
        for pos in (2 * g, 2 * g + 1):
            def got(j, _, pos=pos):
                a2a_copy(pos, j).wait_recv()
                return 0
            lax.fori_loop(1 if SHIFTS[pos] == 0 else 0, 8, got, 0)

    for g in range(3):
        arrive(g)
        tg = group_table(g)

        def remote_part(e, _, g=g, tg=tg):
            rows = pl.ds(pl.multiple_of(e * 256, 256), 256)
            d = dot(onehot[rows, 512 + 256 * g:768 + 256 * g], tg)
            acc2[rows, :] = d if g == 0 else acc2[rows, :] + d
            return 0

        lax.fori_loop(0, EDGES // 256, remote_part, 0)
    arrive(3)
    tg = group_table(3)

    def finish(e, pooled):
        rows = pl.ds(pl.multiple_of(e * 256, 256), 256)
        d = dot(onehot[rows, 1280:1536], tg) + acc2[rows, :]
        pre = acc1[rows, :] + jnp.where(half_b[rows, :].astype(f32) > 0.5, d[:, COLS:], d[:, :COLS])
        return pooled + dot(pool_p[:, rows], silu(pre).astype(bf16))

    pooled = lax.fori_loop(0, EDGES // 256, finish, jnp.zeros((NODES, COLS), f32))
    pool4[ch] = pooled.astype(bf16)
    g_pool = gather_start(pool4, 1)
    for c in g_pool:
        c.wait_recv()
    message = dot(gathered(pool4), msgw[...]).astype(bf16)
    hid4[ch] = silu(self_part + dot(message, inw[...])).astype(bf16)
    g_hid = gather_start(hid4, 2)
    for c in g_hid:
        c.wait_recv()
    update = dot(gathered(hid4), outw[...])
    mean = jnp.mean(update, axis=1, keepdims=True)
    centred = update - mean
    var = jnp.mean(jnp.square(centred), axis=1, keepdims=True)
    upd[...] = gain[...] * centred * lax.rsqrt(var + norm_eps)
    own_cols = pl.ds(pl.multiple_of(ch * COLS, COLS), COLS)
    result = (mine.astype(f32) + upd[:, own_cols]).astype(bf16)
    node_out[...] = result
    for r in range(BAND):
        for m in chunks:
            rows = pl.ds(m * MCH, MCH)
            got = dot(rmat[r, rows, :], result)
            grid_out[r, rows, :] = (x[r, rows, own_cols].astype(f32) + got).astype(bf16)

    halo[0].wait_send()
    halo[1].wait_send()
    for c in g_nodes + g_pool + g_hid:
        c.wait_send()
    for pos in range(8):
        def left(j, _, pos=pos):
            a2a_copy(pos, j).wait_send()
            return 0
        lax.fori_loop(1 if SHIFTS[pos] == 0 else 0, 8, left, 0)


def shards(*args):
    (grid_state, fold_columns, mesh_state, edge_state, conv_weight, conv_bias, source_weight, target_weight,
     edge_weight, edge_bias, message_weight, self_weight, inbox_weight, node_bias, output_weight, output_gain,
     cell_node, cell_weight, edge_source, edge_target, edge_count, send_rows, read_node, read_weight) = args
    anyspace = pl.BlockSpec(memory_space=pl.ANY)
    vmem = pl.BlockSpec(memory_space=pltpu.VMEM)
    V = pltpu.VMEM
    in_specs = [anyspace] * 24
    in_specs[20] = pl.BlockSpec(memory_space=pltpu.SMEM)
    return pl.pallas_call(
        kernel,
        out_shape=(
            jax.ShapeDtypeStruct((NODES, COLS), bf16),
            jax.ShapeDtypeStruct((BAND, LON, COLS), bf16),
        ),
        in_specs=in_specs,
        out_specs=(vmem, vmem),
        scratch_shapes=[
            V((BAND, LON, FEAT), bf16), V((1, LON), i32), V((NODES, COLS), bf16), V((EDGES, FEAT), bf16),
            V((3, FEAT, 3 * COLS), bf16), V((1, COLS), bf16), V((FEAT, COLS), bf16), V((FEAT, COLS), bf16),
            V((FEAT, COLS), bf16), V((1, COLS), bf16),
            V((FEAT, FEAT), bf16), V((FEAT, COLS), bf16), V((FEAT, COLS), bf16), V((1, COLS), bf16),
            V((FEAT, FEAT), bf16), V((1, FEAT), f32), V((BAND, LON), i32), V((BAND, LON), f32),
            V((40, 128), i32), V((40, 128), i32), V((SPACE, CAP), i32), V((3, BAND, LON), i32), V((3, BAND, LON), f32),
            V((LON + 16, 3 * COLS), f32), V((2, LON, COLS), f32), V((2, LON, COLS), bf16), V((2, LON, COLS), bf16),
            V((BAND, LON, COLS), bf16), V((BAND, NODES, LON), bf16), V((SPACE * CAP, 256), bf16),
            V((SPACE, CAP, COLS), bf16), V((512, COLS), bf16),
            V((CHAN, NODES, COLS), bf16), V((CHAN, NODES, COLS), bf16), V((CHAN, NODES, COLS), bf16),
            V((EDGES, 1536), bf16), V((EDGES, 128), bf16), V((NODES, EDGES), bf16),
            V((EDGES, COLS), f32), V((EDGES, 2 * COLS), f32), V((SPACE, CAP, COLS), bf16),
            V((3, 40, 128), i32), V((NODES, LONP), f32), V((BAND, LONP, NODES), bf16), V((NODES, FEAT), f32),
            V((LON, LON), bf16),
            pltpu.SemaphoreType.DMA((40,)), pltpu.SemaphoreType.DMA((2,)), pltpu.SemaphoreType.DMA((2,)),
            pltpu.SemaphoreType.DMA((3, CHAN)), pltpu.SemaphoreType.DMA((3, CHAN)),
            pltpu.SemaphoreType.DMA((SPACE,)), pltpu.SemaphoreType.DMA((SPACE,)),
        ],
        compiler_params=pltpu.CompilerParams(
            collective_id=0, has_side_effects=True, vmem_limit_bytes=60 * 1024 * 1024
        ),
    )(
        grid_state, fold_columns.reshape(1, LON), mesh_state, edge_state, conv_weight, conv_bias.reshape(1, COLS),
        source_weight, target_weight, edge_weight, edge_bias.reshape(1, COLS), message_weight, self_weight,
        inbox_weight, node_bias.reshape(1, COLS), output_weight, output_gain.reshape(1, FEAT), cell_node, cell_weight,
        edge_source.reshape(40, 128), edge_target.reshape(40, 128), edge_count, send_rows, read_node, read_weight,
    )


def solution(mesh):
    in_specs = (
        P("space", None, None), P(), P("space", "chan"), P("space", None), P(None, None, None, "chan"), P("chan"),
        P(None, "chan"), P(None, "chan"), P(None, "chan"), P("chan"), P(), P(None, "chan"), P(None, "chan"), P("chan"),
        P(), P(), P("space", None), P("space", None), P("space"), P("space"), P("space"), P("space", None, None),
        P(None, "space", None), P(None, "space", None),
    )
    out_specs = (P("space", "chan"), P("space", None, "chan"))
    return jax.shard_map(shards, mesh=mesh, in_specs=in_specs, out_specs=out_specs, check_vma=False)
```

```python
import jax
import jax.numpy as jnp
from jax import lax
from jax.experimental import pallas as pl
from jax.experimental.pallas import tpu as pltpu
from jax.sharding import PartitionSpec as P

f32 = jnp.float32
bf16 = jnp.bfloat16
i32 = jnp.int32
norm_eps = 1e-05
MESH = pl.DeviceIdType.MESH

SPACE, CHAN = 64, 4
NY, NZ, NX = 2, 8, 4
FEAT, COLS = 512, 128
BAND, LON = 3, 720
NODES = 160
EDGES = 5120
CAP = 32
MCH = 240
LONP = 768
SHIFTS = (0, 4, 3, 5, 2, 6, 1, 7)
ECH = 1280
UNROLL = 4


def dot(a, b):
    return jnp.dot(a, b, preferred_element_type=f32)


def silu(v):
    return 0.5 * v * (1.0 + jnp.tanh(0.5 * v))


def kernel(
    grid_h, fold_h, mesh_h, edge_h, convw_h, convb_h, srcw_h, tgtw_h, edgew_h, edgeb_h,
    msgw_h, selfw_h, inw_h, nodeb_h, outw_h, gain_h, celln_h, cellw_h, esrc_h, etgt_h,
    ecount, send_h, readn_h, readw_h,
    node_out, rmat_h,
    x, fold, mesh_v, edge, wcat, convb, srcw, tgtw, edgew, edgeb,
    msgw, selfw, inw, nodeb, outw, gain, celln, cellw, esrc, etgt, sendr, readn, readw,
    z, cpart, halo_out, halo_in, act, inc_a, sel_o, outg, table, nodes4, pool4, hid4,
    onehot, half_b, pool_p, acc1, acc2, incoming, ridx, rwt, rmat, upd, srcc,
    load_sem, halo_send, halo_recv, gat_send, gat_recv, a2a_send, a2a_recv, rmat_sem, near_sem,
):
    me = lax.axis_index("space")
    ch = lax.axis_index("chan")
    my, mz, mx = me // 32, (me // 4) % 8, me % 4

    loads = {}

    def load(name, src, dst):
        k = len(loads)
        c = pltpu.make_async_copy(src, dst, load_sem.at[k])
        c.start()
        loads[name] = c

    def ready(*names):
        for name in names:
            loads[name].wait()

    def load_w(a):
        for b in range(3):
            load(("w", a, b), convw_h.at[a, b], wcat.at[a, :, b * COLS:(b + 1) * COLS])

    load("x0", grid_h.at[0], x.at[0])
    load_w(2)

    barrier = pltpu.get_barrier_semaphore()

    def hail(sem, **where):
        pl.semaphore_signal(sem, inc=1, device_id=where, device_id_type=MESH)

    def at(dy, dz, dx):
        return ((my + dy) % NY) * 32 + ((mz + dz) % NZ) * 4 + (mx + dx) % NX

    hail(barrier, space=(me + 1) % SPACE)
    hail(barrier, space=(me + SPACE - 1) % SPACE)
    for d in range(1, CHAN):
        hail(barrier, chan=(ch + d) % CHAN)
    hail(barrier, space=at(1, 0, 0))
    for d in range(1, NX):
        hail(barrier, space=at(0, 0, d))
    for d in range(1, NZ):
        hail(barrier, space=at(0, d, 0))
    load("x2", grid_h.at[2], x.at[2])
    load_w(0)
    load("x1", grid_h.at[1], x.at[1])
    load_w(1)
    for name, s, d in (
        ("convb", convb_h, convb), ("celln", celln_h, celln), ("cellw", cellw_h, cellw),
        ("sendr", send_h.at[0], sendr), ("esrc", esrc_h, esrc), ("etgt", etgt_h, etgt),
        ("fold", fold_h, fold), ("mesh", mesh_h, mesh_v), ("srcw", srcw_h, srcw), ("tgtw", tgtw_h, tgtw),
        ("edgew", edgew_h, edgew), ("edgeb", edgeb_h, edgeb),
        ("e0", edge_h.at[0:2560], edge.at[0:2560]), ("e1", edge_h.at[2560:5120], edge.at[2560:5120]),
        ("selfw", selfw_h, selfw), ("msgw", msgw_h, msgw), ("inw", inw_h, inw), ("nodeb", nodeb_h, nodeb),
        ("outw", outw_h, outw), ("gain", gain_h, gain), ("readn", readn_h, readn), ("readw", readw_h, readw),
    ):
        load(name, s, d)

    def conv_z(terms):
        for m in range(LON // MCH):
            rows = pl.ds(m * MCH, MCH)
            acc = None
            for xr, a in terms:
                d = dot(xr[rows, :], wcat[a])
                acc = d if acc is None else acc + d
            z[pl.ds(8 + m * MCH, MCH), :] = acc
        z[7:8, 0:COLS] = z[LON + 7:LON + 8, 0:COLS]
        z[LON + 8:LON + 9, 2 * COLS:3 * COLS] = z[8:9, 2 * COLS:3 * COLS]

    def shifted(m):
        o = m * MCH
        return (
            z[pl.ds(o + 7, MCH), 0:COLS]
            + z[pl.ds(o + 8, MCH), COLS:2 * COLS]
            + z[pl.ds(o + 9, MCH), 2 * COLS:3 * COLS]
        )

    chunks = range(LON // MCH)

    ready("x0", ("w", 2, 0), ("w", 2, 1), ("w", 2, 2))
    conv_z([(x.at[0], 2)])
    for m in chunks:
        halo_out[0, pl.ds(m * MCH, MCH), :] = shifted(m).astype(bf16)
    pl.semaphore_wait(barrier, 2 + CHAN - 1 + NY - 1 + NX - 1 + NZ - 1)
    for d in range(1, NX):
        hail(near_sem.at[0], space=at(0, 0, d))

    def halo_copy(k):
        peer = (me + SPACE - 1) % SPACE if k == 0 else (me + 1) % SPACE
        return pltpu.make_async_remote_copy(
            src_ref=halo_out.at[k], dst_ref=halo_in.at[k], send_sem=halo_send.at[k], recv_sem=halo_recv.at[k],
            device_id={"space": peer}, device_id_type=MESH,
        )

    halo = [halo_copy(0), halo_copy(1)]
    halo[0].start()
    ready("x2", ("w", 0, 0), ("w", 0, 1), ("w", 0, 2))
    conv_z([(x.at[2], 0)])
    for m in chunks:
        halo_out[1, pl.ds(m * MCH, MCH), :] = shifted(m).astype(bf16)
    halo[1].start()
    pl.semaphore_wait(near_sem.at[0], NX - 1)
    hail(near_sem.at[1], space=at(1, 0, 0))

    ready("x1", ("w", 1, 0), ("w", 1, 1), ("w", 1, 2), "convb", "celln", "cellw")
    bias = convb[...].astype(f32)
    for r, terms in (
        (0, [(x.at[0], 1), (x.at[1], 2)]),
        (2, [(x.at[1], 0), (x.at[2], 1)]),
        (1, [(x.at[0], 0), (x.at[1], 1), (x.at[2], 2)]),
    ):
        conv_z(terms)
        for m in chunks:
            v = shifted(m) + bias
            rows = pl.ds(m * MCH, MCH)
            if r == 1:
                act[1, rows, :] = silu(v).astype(bf16)
            else:
                cpart[r // 2, rows, :] = v

    ready("fold")

    @pl.when(me == SPACE - 1)
    def _():
        def body(t, _):
            rows = pl.ds(pl.multiple_of(t * 16, 16), 16)
            ids = lax.broadcasted_iota(i32, (16, LON), 0) + t * 16
            pick = jnp.where(ids == fold[...].reshape(1, LON), 1.0, 0.0).astype(bf16)
            srcc[rows, :] = pick
            return 0

        lax.fori_loop(0, LON // 16, body, 0)
        xf = lax.dot_general(srcc[...], x[2], (((0,), (0,)), ((), ())), preferred_element_type=f32)
        upd_x = xf.astype(bf16)
        onehot[0:LON, 0:FEAT] = upd_x
        conv_z([(onehot.at[0:LON, 0:FEAT], 2)])
        for m in chunks:
            rows = pl.ds(m * MCH, MCH)
            cpart[1, rows, :] = cpart[1, rows, :] + shifted(m)

    for r in range(BAND):
        ids = lax.broadcasted_iota(i32, (NODES, LON), 0)
        inc_a[r] = jnp.where(ids == celln[r:r + 1, :], cellw[r:r + 1, :], 0.0).astype(bf16)

    ready("sendr", "esrc", "etgt")
    send_t = sendr[...].astype(f32)
    lane256 = lax.broadcasted_iota(i32, (CAP, 256), 1).astype(f32)
    for p in range(SPACE):
        sel_o[p * CAP:(p + 1) * CAP, :] = jnp.where(send_t[:, p:p + 1] == lane256, 1.0, 0.0).astype(bf16)

    s = esrc[...]
    u = s - NODES
    q = lax.shift_right_logical(u, 5) & 63
    k = u & 31
    dz = (mz - (lax.shift_right_logical(q, 2) & 7)) & 7
    dy = (my - lax.shift_right_logical(q, 5)) & 1
    dx = (mx - (q & 3)) & 3
    t = jnp.zeros_like(s)
    for pos, shift in enumerate(SHIFTS):
        t = jnp.where(dz == shift, pos, t)
    remote = 256 + lax.shift_right_logical(t, 1) * 256 + (dy * 4 + dx) * CAP + k
    col = jnp.where(u < 0, s, remote)
    halfbit = jnp.where(u < 0, 0, t & 1)
    slot = lax.broadcasted_iota(i32, s.shape, 0) * 128 + lax.broadcasted_iota(i32, s.shape, 1)
    live_t = jnp.where(slot < ecount[0], etgt[...], -1)
    srcc2 = col + 2048 * halfbit
    ridx[0] = srcc2
    ridx[1] = etgt[...]
    ridx[2] = live_t

    lane_f = lax.broadcasted_iota(i32, (128, 128), 1).astype(f32)

    def column(which, e):
        row = ridx[which, pl.ds(e, 1), :].astype(f32)
        return jnp.broadcast_to(row, (128, 128)).T

    def build_one(e):
        rows = pl.ds(pl.multiple_of(e * 128, 128), 128)
        c = column(0, e)
        hb = jnp.where(c >= 2048.0, 1.0, 0.0)
        half_b[rows, :] = hb.astype(bf16)
        c = c - 2048.0 * hb
        hi = jnp.floor(c * (1.0 / 128.0))
        lo = c - 128.0 * hi
        m = jnp.where(lo == lane_f, hi, -1.0).astype(bf16)
        one = jnp.ones((128, 128), bf16)
        zero = jnp.zeros((128, 128), bf16)
        for tile in range(10):
            to = tile if tile < 2 else tile + 2
            onehot[rows, to * 128:(to + 1) * 128] = jnp.where(m == jnp.asarray(tile, bf16), one, zero)
        c = column(1, e)
        for tile in range(2):
            onehot[rows, (2 + tile) * 128:(3 + tile) * 128] = jnp.where(
                c == lane_f + 128.0 * tile, 1.0, 0.0
            ).astype(bf16)
        ids = lax.broadcasted_iota(i32, (NODES, 128), 0)
        pool_p[:, rows] = jnp.where(ids == ridx[2, pl.ds(e, 1), :], 1.0, 0.0).astype(bf16)

    def build(b, _):
        for k in range(UNROLL):
            build_one(b * UNROLL + k)
        return 0

    BUILDS = EDGES // 128 // UNROLL
    FIRST = BUILDS // 2
    lax.fori_loop(0, FIRST, build, 0)

    halo[0].wait_recv()
    halo[1].wait_recv()
    south_ok = jnp.where(me > 0, 1.0, 0.0)
    north_ok = jnp.where(me < SPACE - 1, 1.0, 0.0)
    for m in chunks:
        rows = pl.ds(m * MCH, MCH)
        act[0, rows, :] = silu(cpart[0, rows, :] + halo_in[1, rows, :].astype(f32) * south_ok).astype(bf16)
        act[2, rows, :] = silu(cpart[1, rows, :] + halo_in[0, rows, :].astype(f32) * north_ok).astype(bf16)
    ready("mesh")
    agg = dot(inc_a[0], act[0]) + dot(inc_a[1], act[1]) + dot(inc_a[2], act[2])
    mine = (mesh_v[...].astype(f32) + agg).astype(bf16)

    def gather_start(buf, stage):
        out = []
        for d in range(1, CHAN):
            c = pltpu.make_async_remote_copy(
                src_ref=buf.at[ch], dst_ref=buf.at[ch],
                send_sem=gat_send.at[stage, d], recv_sem=gat_recv.at[stage, d],
                device_id={"chan": (ch + d) % CHAN}, device_id_type=MESH,
            )
            c.start()
            out.append(c)
        return out

    def gathered(buf):
        return jnp.concatenate([buf[0], buf[1], buf[2], buf[3]], axis=1)

    nodes4[ch] = mine
    g_nodes = gather_start(nodes4, 0)
    ready("srcw", "tgtw")
    lax.fori_loop(FIRST, BUILDS, build, 0)
    for c in g_nodes:
        c.wait_recv()
    nodes = gathered(nodes4)
    sent = dot(nodes, srcw[...]).astype(bf16)
    table[...] = jnp.zeros_like(table)
    table[0:NODES, :] = sent
    for b in range(SPACE * CAP // 256):
        picked = dot(sel_o[b * 256:(b + 1) * 256, :], table[0:256, :]).astype(bf16)
        outg[b * 8:(b + 1) * 8] = picked.reshape(8, CAP, COLS)

    def a2a_copy(pos, j):
        peer = at(j // 4, SHIFTS[pos], j % 4)
        sl = pos * 8 + j
        return pltpu.make_async_remote_copy(
            src_ref=outg.at[peer], dst_ref=incoming.at[sl], send_sem=a2a_send.at[0], recv_sem=a2a_recv.at[pos // 2],
            device_id={"space": peer}, device_id_type=MESH,
        )

    def slots(first, count, group):
        part = incoming.at[pl.ds(first, count)]
        return pltpu.make_async_remote_copy(
            src_ref=outg.at[pl.ds(first, count)], dst_ref=part, send_sem=a2a_send.at[0], recv_sem=a2a_recv.at[group],
            device_id={"space": (me + 1) % SPACE}, device_id_type=MESH,
        )

    pl.semaphore_wait(near_sem.at[1], 1)
    for pos in (1, 0, 2, 3, 4, 5, 6, 7):
        def go(j, _, pos=pos):
            a2a_copy(pos, j).start()
            return 0
        lax.fori_loop(1 if SHIFTS[pos] == 0 else 0, 8, go, 0)
    incoming[0] = outg[me]

    table[256:256 + NODES, :] = dot(nodes, tgtw[...]).astype(bf16)
    ready("edgew", "edgeb", "e0", "e1")
    ebias = edgeb[...].astype(f32)

    def own(e, _):
        rows = pl.ds(pl.multiple_of(e * ECH, ECH), ECH)
        acc1[rows, :] = dot(edge[rows, :], edgew[...]) + dot(onehot[rows, 0:512], table[...]) + ebias
        return 0

    lax.fori_loop(0, EDGES // ECH, own, 0)

    ready("selfw", "nodeb", "readn", "readw", "msgw", "inw", "outw", "gain")
    self_part = dot(nodes, selfw[...]) + nodeb[...].astype(f32)
    ids = lax.broadcasted_iota(i32, (NODES, LON), 0)
    for r in range(BAND):
        w = jnp.zeros((NODES, LON), f32)
        for corner in range(3):
            w = w + jnp.where(ids == readn[corner, r:r + 1, :], readw[corner, r:r + 1, :], 0.0)
        rwt[:, 0:LON] = w
        rwt[:, LON:LONP] = jnp.zeros((NODES, LONP - LON), f32)
        for tile in range(LONP // 128):
            rmat[r, tile * 128:(tile + 1) * 128, :] = rwt[:, tile * 128:(tile + 1) * 128].T.astype(bf16)
    rmat_copy = pltpu.make_async_copy(rmat, rmat_h, rmat_sem.at[0])
    rmat_copy.start()

    def group_table(g):
        left = incoming[16 * g:16 * g + 8].reshape(256, COLS)
        right = incoming[16 * g + 8:16 * g + 16].reshape(256, COLS)
        return jnp.concatenate([left, right], axis=1)

    def arrive(g):
        first = 1 if g == 0 else 0
        slots(16 * g + first, 16 - first, g).wait_recv()

    for g in range(3):
        arrive(g)
        tg = group_table(g)

        def remote_part(e, _, g=g, tg=tg):
            rows = pl.ds(pl.multiple_of(e * ECH, ECH), ECH)
            d = dot(onehot[rows, 512 + 256 * g:768 + 256 * g], tg)
            acc2[rows, :] = d if g == 0 else acc2[rows, :] + d
            return 0

        lax.fori_loop(0, EDGES // ECH, remote_part, 0)
    arrive(3)
    tg = group_table(3)

    def finish(e, pooled):
        rows = pl.ds(pl.multiple_of(e * ECH, ECH), ECH)
        d = dot(onehot[rows, 1280:1536], tg) + acc2[rows, :]
        pre = acc1[rows, :] + jnp.where(half_b[rows, :].astype(f32) > 0.5, d[:, COLS:], d[:, :COLS])
        return pooled + dot(pool_p[:, rows], silu(pre).astype(bf16))

    pooled = lax.fori_loop(0, EDGES // ECH, finish, jnp.zeros((NODES, COLS), f32))
    pool4[ch] = pooled.astype(bf16)
    g_pool = gather_start(pool4, 1)
    for c in g_pool:
        c.wait_recv()
    message = dot(gathered(pool4), msgw[...]).astype(bf16)
    hid4[ch] = silu(self_part + dot(message, inw[...])).astype(bf16)
    g_hid = gather_start(hid4, 2)
    for c in g_hid:
        c.wait_recv()
    update = dot(gathered(hid4), outw[...])
    mean = jnp.mean(update, axis=1, keepdims=True)
    centred = update - mean
    var = jnp.mean(jnp.square(centred), axis=1, keepdims=True)
    upd[...] = gain[...] * centred * lax.rsqrt(var + norm_eps)
    own_cols = pl.ds(pl.multiple_of(ch * COLS, COLS), COLS)
    result = (mine.astype(f32) + upd[:, own_cols]).astype(bf16)
    node_out[...] = result

    halo[0].wait_send()
    halo[1].wait_send()
    for c in g_nodes + g_pool + g_hid:
        c.wait_send()
    slots(0, SPACE - 1, 0).wait_send()
    rmat_copy.wait()


def read_back(grid_h, rmat, node_h, node_o, grid_o, x, out, sem):
    ch = lax.axis_index("chan")
    own_cols = pl.ds(pl.multiple_of(ch * COLS, COLS), COLS)
    bands = [pltpu.make_async_copy(grid_h.at[r, :, own_cols], x.at[r], sem.at[r]) for r in range(BAND)]
    for c in bands:
        c.start()
    node_copy = pltpu.make_async_copy(node_h, node_o, sem.at[6])
    node_copy.start()
    result = node_h[...]
    done = []
    for r in range(BAND):
        bands[r].wait()
        for m in range(LON // MCH):
            rows = pl.ds(m * MCH, MCH)
            out[r, rows, :] = (x[r, rows, :].astype(f32) + dot(rmat[r, rows, :], result)).astype(bf16)
        c = pltpu.make_async_copy(out.at[r], grid_o.at[r], sem.at[3 + r])
        c.start()
        done.append(c)
    for c in done + [node_copy]:
        c.wait()


def shards(*args):
    (grid_state, fold_columns, mesh_state, edge_state, conv_weight, conv_bias, source_weight, target_weight,
     edge_weight, edge_bias, message_weight, self_weight, inbox_weight, node_bias, output_weight, output_gain,
     cell_node, cell_weight, edge_source, edge_target, edge_count, send_rows, read_node, read_weight) = args
    anyspace = pl.BlockSpec(memory_space=pl.ANY)
    vmem = pl.BlockSpec(memory_space=pltpu.VMEM)
    V = pltpu.VMEM
    in_specs = [anyspace] * 24
    in_specs[20] = pl.BlockSpec(memory_space=pltpu.SMEM)
    result, rmat = pl.pallas_call(
        kernel,
        out_shape=(
            jax.ShapeDtypeStruct((NODES, COLS), bf16),
            jax.ShapeDtypeStruct((BAND, LONP, NODES), bf16),
        ),
        in_specs=in_specs,
        out_specs=(vmem, anyspace),
        scratch_shapes=[
            V((BAND, LON, FEAT), bf16), V((LON,), i32), V((NODES, COLS), bf16), V((EDGES, FEAT), bf16),
            V((3, FEAT, 3 * COLS), bf16), V((1, COLS), bf16), V((FEAT, COLS), bf16), V((FEAT, COLS), bf16),
            V((FEAT, COLS), bf16), V((1, COLS), bf16),
            V((FEAT, FEAT), bf16), V((FEAT, COLS), bf16), V((FEAT, COLS), bf16), V((1, COLS), bf16),
            V((FEAT, FEAT), bf16), V((1, FEAT), f32), V((BAND, LON), i32), V((BAND, LON), f32),
            V((40, 128), i32), V((40, 128), i32), V((CAP, SPACE), i32), V((3, BAND, LON), i32), V((3, BAND, LON), f32),
            V((LON + 16, 3 * COLS), f32), V((2, LON, COLS), f32), V((2, LON, COLS), bf16), V((2, LON, COLS), bf16),
            V((BAND, LON, COLS), bf16), V((BAND, NODES, LON), bf16), V((SPACE * CAP, 256), bf16),
            V((SPACE, CAP, COLS), bf16), V((512, COLS), bf16),
            V((CHAN, NODES, COLS), bf16), V((CHAN, NODES, COLS), bf16), V((CHAN, NODES, COLS), bf16),
            V((EDGES, 1536), bf16), V((EDGES, 128), bf16), V((NODES, EDGES), bf16),
            V((EDGES, COLS), f32), V((EDGES, 2 * COLS), f32), V((SPACE, CAP, COLS), bf16),
            V((3, 40, 128), i32), V((NODES, LONP), f32), V((BAND, LONP, NODES), bf16), V((NODES, FEAT), f32),
            V((LON, LON), bf16),
            pltpu.SemaphoreType.DMA((40,)), pltpu.SemaphoreType.DMA((2,)), pltpu.SemaphoreType.DMA((2,)),
            pltpu.SemaphoreType.DMA((3, CHAN)), pltpu.SemaphoreType.DMA((3, CHAN)),
            pltpu.SemaphoreType.DMA((1,)), pltpu.SemaphoreType.DMA((4,)), pltpu.SemaphoreType.DMA((1,)),
            pltpu.SemaphoreType.REGULAR((2,)),
        ],
        compiler_params=pltpu.CompilerParams(
            collective_id=0, has_side_effects=True, vmem_limit_bytes=60 * 1024 * 1024
        ),
    )(
        grid_state, fold_columns, mesh_state, edge_state, conv_weight, conv_bias.reshape(1, COLS),
        source_weight, target_weight, edge_weight, edge_bias.reshape(1, COLS), message_weight, self_weight,
        inbox_weight, node_bias.reshape(1, COLS), output_weight, output_gain.reshape(1, FEAT), cell_node, cell_weight,
        edge_source.reshape(40, 128), edge_target.reshape(40, 128), edge_count, send_rows.transpose(0, 2, 1), read_node, read_weight,
    )
    return pl.pallas_call(
        read_back,
        out_shape=(
            jax.ShapeDtypeStruct((NODES, COLS), bf16),
            jax.ShapeDtypeStruct((BAND, LON, COLS), bf16),
        ),
        in_specs=[anyspace, vmem, vmem],
        out_specs=(anyspace, anyspace),
        scratch_shapes=[V((BAND, LON, COLS), bf16), V((BAND, LON, COLS), bf16), pltpu.SemaphoreType.DMA((7,))],
    )(grid_state, rmat, result)


def solution(mesh):
    in_specs = (
        P("space", None, None), P(), P("space", "chan"), P("space", None), P(None, None, None, "chan"), P("chan"),
        P(None, "chan"), P(None, "chan"), P(None, "chan"), P("chan"), P(), P(None, "chan"), P(None, "chan"), P("chan"),
        P(), P(), P("space", None), P("space", None), P("space"), P("space"), P("space"), P("space", None, None),
        P(None, "space", None), P(None, "space", None),
    )
    out_specs = (P("space", "chan"), P("space", None, "chan"))
    return jax.shard_map(shards, mesh=mesh, in_specs=in_specs, out_specs=out_specs, check_vma=False)
```

```python
import jax
import jax.numpy as jnp
from jax import lax
from jax.experimental import pallas as pl
from jax.experimental.pallas import tpu as pltpu
from jax.sharding import PartitionSpec as P

f32 = jnp.float32
bf16 = jnp.bfloat16
i32 = jnp.int32
norm_eps = 1e-05
MESH = pl.DeviceIdType.MESH

SPACE, CHAN = 64, 4
NY, NZ, NX = 2, 8, 4
FEAT, COLS = 512, 128
BAND, LON = 3, 720
NODES = 160
EDGES = 5120
CAP = 32
MCH = 240
LONP = 768
SHIFTS = (0, 4, 3, 5, 2, 6, 1, 7)
ECH = 1280
UNROLL = 4
EARLY = 4


def dot(a, b):
    return jnp.dot(a, b, preferred_element_type=f32)


def silu(v):
    return 0.5 * v * (1.0 + jnp.tanh(0.5 * v))


def kernel(
    grid_h, fold_h, mesh_h, edge_h, convw_h, convb_h, srcw_h, tgtw_h, edgew_h, edgeb_h,
    msgw_h, selfw_h, inw_h, nodeb_h, outw_h, gain_h, celln_h, cellw_h, esrc_h, etgt_h,
    ecount, send_h, readn_h, readw_h,
    node_out, rmat_h,
    x, fold, mesh_v, edge, wcat, convb, srcw, tgtw, edgew, edgeb,
    msgw, selfw, inw, nodeb, outw, gain, celln, cellw, esrc, etgt, sendr, readn, readw,
    z, cpart, halo_out, halo_in, act, inc_a, sel_o, outg, table, nodes4, pool4, hid4,
    onehot, half_b, pool_p, acc1, acc2, incoming, ridx, rwt, rmat, upd, srcc,
    load_sem, halo_send, halo_recv, gat_send, gat_recv, a2a_send, a2a_recv, rmat_sem, near_sem,
):
    me = lax.axis_index("space")
    ch = lax.axis_index("chan")
    my, mz, mx = me // 32, (me // 4) % 8, me % 4

    loads = {}

    def load(name, src, dst):
        k = len(loads)
        c = pltpu.make_async_copy(src, dst, load_sem.at[k])
        c.start()
        loads[name] = c

    def ready(*names):
        for name in names:
            loads[name].wait()

    def load_w(a):
        for b in range(3):
            load(("w", a, b), convw_h.at[a, b], wcat.at[a, :, b * COLS:(b + 1) * COLS])

    load("x0", grid_h.at[0], x.at[0])
    load_w(2)
    load("x2", grid_h.at[2], x.at[2])
    load_w(0)
    load("x1", grid_h.at[1], x.at[1])
    load_w(1)

    barrier = pltpu.get_barrier_semaphore()

    def hail(sem, **where):
        pl.semaphore_signal(sem, inc=1, device_id=where, device_id_type=MESH)

    y_at = [((my + d) % NY) * 32 for d in range(NY)]
    z_at = [((mz + d) % NZ) * 4 for d in range(NZ)]
    x_at = [(mx + d) % NX for d in range(NX)]

    def at(dy, dz, dx):
        return y_at[dy] + z_at[dz] + x_at[dx]

    hail(barrier, space=(me + 1) % SPACE)
    hail(barrier, space=(me + SPACE - 1) % SPACE)
    for d in range(1, CHAN):
        hail(barrier, chan=(ch + d) % CHAN)
    hail(barrier, space=at(1, 0, 0))
    for d in range(1, NX):
        hail(barrier, space=at(0, 0, d))
    for d in range(1, NZ):
        hail(barrier, space=at(0, d, 0))
    for name, s, d in (
        ("convb", convb_h, convb), ("celln", celln_h, celln), ("cellw", cellw_h, cellw),
        ("sendr", send_h.at[0], sendr), ("fold", fold_h, fold), ("mesh", mesh_h, mesh_v), ("srcw", srcw_h, srcw),
    ):
        load(name, s, d)

    def conv_z(terms):
        for m in range(LON // MCH):
            rows = pl.ds(m * MCH, MCH)
            acc = None
            for xr, a in terms:
                d = dot(xr[rows, :], wcat[a])
                acc = d if acc is None else acc + d
            z[pl.ds(8 + m * MCH, MCH), :] = acc
        z[7:8, 0:COLS] = z[LON + 7:LON + 8, 0:COLS]
        z[LON + 8:LON + 9, 2 * COLS:3 * COLS] = z[8:9, 2 * COLS:3 * COLS]

    def shifted(m):
        o = m * MCH
        return (
            z[pl.ds(o + 7, MCH), 0:COLS]
            + z[pl.ds(o + 8, MCH), COLS:2 * COLS]
            + z[pl.ds(o + 9, MCH), 2 * COLS:3 * COLS]
        )

    chunks = range(LON // MCH)

    ready("x0", ("w", 2, 0), ("w", 2, 1), ("w", 2, 2))
    conv_z([(x.at[0], 2)])
    for m in chunks:
        halo_out[0, pl.ds(m * MCH, MCH), :] = shifted(m).astype(bf16)
    pl.semaphore_wait(barrier, 2 + CHAN - 1 + NY - 1 + NX - 1 + NZ - 1)
    for d in range(1, NX):
        hail(near_sem.at[0], space=at(0, 0, d))

    def halo_copy(k):
        peer = (me + SPACE - 1) % SPACE if k == 0 else (me + 1) % SPACE
        return pltpu.make_async_remote_copy(
            src_ref=halo_out.at[k], dst_ref=halo_in.at[k], send_sem=halo_send.at[k], recv_sem=halo_recv.at[k],
            device_id={"space": peer}, device_id_type=MESH,
        )

    halo = [halo_copy(0), halo_copy(1)]
    halo[0].start()
    ready("x2", ("w", 0, 0), ("w", 0, 1), ("w", 0, 2))
    conv_z([(x.at[2], 0)])
    for m in chunks:
        halo_out[1, pl.ds(m * MCH, MCH), :] = shifted(m).astype(bf16)
    halo[1].start()
    pl.semaphore_wait(near_sem.at[0], NX - 1)
    hail(near_sem.at[1], space=at(1, 0, 0))

    ready("x1", ("w", 1, 0), ("w", 1, 1), ("w", 1, 2), "convb", "celln", "cellw")
    for name, s, d in (
        ("esrc", esrc_h, esrc), ("etgt", etgt_h, etgt), ("tgtw", tgtw_h, tgtw),
        ("edgew", edgew_h, edgew), ("edgeb", edgeb_h, edgeb),
        ("e0", edge_h.at[0:2560], edge.at[0:2560]), ("e1", edge_h.at[2560:5120], edge.at[2560:5120]),
        ("selfw", selfw_h, selfw), ("msgw", msgw_h, msgw), ("inw", inw_h, inw), ("nodeb", nodeb_h, nodeb),
        ("outw", outw_h, outw), ("gain", gain_h, gain), ("readn", readn_h, readn), ("readw", readw_h, readw),
    ):
        load(name, s, d)
    bias = convb[...].astype(f32)
    for r, terms in (
        (0, [(x.at[0], 1), (x.at[1], 2)]),
        (2, [(x.at[1], 0), (x.at[2], 1)]),
        (1, [(x.at[0], 0), (x.at[1], 1), (x.at[2], 2)]),
    ):
        conv_z(terms)
        for m in chunks:
            v = shifted(m) + bias
            rows = pl.ds(m * MCH, MCH)
            if r == 1:
                act[1, rows, :] = silu(v).astype(bf16)
            else:
                cpart[r // 2, rows, :] = v

    ready("fold")

    @pl.when(me == SPACE - 1)
    def _():
        def body(t, _):
            rows = pl.ds(pl.multiple_of(t * 16, 16), 16)
            ids = lax.broadcasted_iota(i32, (16, LON), 0) + t * 16
            pick = jnp.where(ids == fold[...].reshape(1, LON), 1.0, 0.0).astype(bf16)
            srcc[rows, :] = pick
            return 0

        lax.fori_loop(0, LON // 16, body, 0)
        xf = lax.dot_general(srcc[...], x[2], (((0,), (0,)), ((), ())), preferred_element_type=f32)
        upd_x = xf.astype(bf16)
        onehot[0:LON, 0:FEAT] = upd_x
        conv_z([(onehot.at[0:LON, 0:FEAT], 2)])
        for m in chunks:
            rows = pl.ds(m * MCH, MCH)
            cpart[1, rows, :] = cpart[1, rows, :] + shifted(m)

    for r in range(BAND):
        ids = lax.broadcasted_iota(i32, (NODES, LON), 0)
        inc_a[r] = jnp.where(ids == celln[r:r + 1, :], cellw[r:r + 1, :], 0.0).astype(bf16)

    ready("sendr")
    send_t = sendr[...].astype(f32)
    lane256 = lax.broadcasted_iota(i32, (CAP, 256), 1).astype(f32)
    for p in range(SPACE):
        sel_o[p * CAP:(p + 1) * CAP, :] = jnp.where(send_t[:, p:p + 1] == lane256, 1.0, 0.0).astype(bf16)

    halo[0].wait_recv()
    halo[1].wait_recv()
    south_ok = jnp.where(me > 0, 1.0, 0.0)
    north_ok = jnp.where(me < SPACE - 1, 1.0, 0.0)
    for m in chunks:
        rows = pl.ds(m * MCH, MCH)
        act[0, rows, :] = silu(cpart[0, rows, :] + halo_in[1, rows, :].astype(f32) * south_ok).astype(bf16)
        act[2, rows, :] = silu(cpart[1, rows, :] + halo_in[0, rows, :].astype(f32) * north_ok).astype(bf16)
    ready("mesh")
    agg = dot(inc_a[0], act[0]) + dot(inc_a[1], act[1]) + dot(inc_a[2], act[2])
    mine = (mesh_v[...].astype(f32) + agg).astype(bf16)

    def gather_start(buf, stage):
        out = []
        for d in range(1, CHAN):
            c = pltpu.make_async_remote_copy(
                src_ref=buf.at[ch], dst_ref=buf.at[ch],
                send_sem=gat_send.at[stage, d], recv_sem=gat_recv.at[stage, d],
                device_id={"chan": (ch + d) % CHAN}, device_id_type=MESH,
            )
            c.start()
            out.append(c)
        return out

    def gathered(buf):
        return jnp.concatenate([buf[0], buf[1], buf[2], buf[3]], axis=1)

    nodes4[ch] = mine
    g_nodes = gather_start(nodes4, 0)
    ready("srcw", "tgtw")
    table[...] = jnp.zeros_like(table)

    ready("esrc", "etgt")
    s = esrc[...]
    u = s - NODES
    q = lax.shift_right_logical(u, 5) & 63
    k = u & 31
    dz = (mz - (lax.shift_right_logical(q, 2) & 7)) & 7
    dy = (my - lax.shift_right_logical(q, 5)) & 1
    dx = (mx - (q & 3)) & 3
    t = jnp.zeros_like(s)
    for pos, shift in enumerate(SHIFTS):
        t = jnp.where(dz == shift, pos, t)
    remote = 256 + lax.shift_right_logical(t, 1) * 256 + (dy * 4 + dx) * CAP + k
    col = jnp.where(u < 0, s, remote)
    halfbit = jnp.where(u < 0, 0, t & 1)
    slot = lax.broadcasted_iota(i32, s.shape, 0) * 128 + lax.broadcasted_iota(i32, s.shape, 1)
    live_t = jnp.where(slot < ecount[0], etgt[...], -1)
    srcc2 = col + 2048 * halfbit
    ridx[0] = srcc2
    ridx[1] = etgt[...]
    ridx[2] = live_t

    lane_f = lax.broadcasted_iota(i32, (128, 128), 1).astype(f32)

    def column(which, e):
        row = ridx[which, pl.ds(e, 1), :].astype(f32)
        return jnp.broadcast_to(row, (128, 128)).T

    def build_one(e):
        rows = pl.ds(pl.multiple_of(e * 128, 128), 128)
        c = column(0, e)
        hb = jnp.where(c >= 2048.0, 1.0, 0.0)
        half_b[rows, :] = hb.astype(bf16)
        c = c - 2048.0 * hb
        hi = jnp.floor(c * (1.0 / 128.0))
        lo = c - 128.0 * hi
        m = jnp.where(lo == lane_f, hi, -1.0).astype(bf16)
        one = jnp.ones((128, 128), bf16)
        zero = jnp.zeros((128, 128), bf16)
        for tile in range(10):
            to = tile if tile < 2 else tile + 2
            onehot[rows, to * 128:(to + 1) * 128] = jnp.where(m == jnp.asarray(tile, bf16), one, zero)
        c = column(1, e)
        for tile in range(2):
            onehot[rows, (2 + tile) * 128:(3 + tile) * 128] = jnp.where(
                c == lane_f + 128.0 * tile, 1.0, 0.0
            ).astype(bf16)
        ids = lax.broadcasted_iota(i32, (NODES, 128), 0)
        pool_p[:, rows] = jnp.where(ids == ridx[2, pl.ds(e, 1), :], 1.0, 0.0).astype(bf16)

    def build(b, _):
        for k in range(UNROLL):
            build_one(b * UNROLL + k)
        return 0

    BUILDS = EDGES // 128 // UNROLL
    lax.fori_loop(0, EARLY, build, 0)
    for c in g_nodes:
        c.wait_recv()
    nodes = gathered(nodes4)
    sent = dot(nodes, srcw[...]).astype(bf16)
    table[0:NODES, :] = sent
    for b in range(SPACE * CAP // 256):
        picked = dot(sel_o[b * 256:(b + 1) * 256, :], table[0:256, :]).astype(bf16)
        outg[b * 8:(b + 1) * 8] = picked.reshape(8, CAP, COLS)

    def a2a_copy(pos, j):
        peer = y_at[j // 4] + z_at[SHIFTS[pos]] + x_at[j % 4]
        sl = pos * 8 + j
        return pltpu.make_async_remote_copy(
            src_ref=outg.at[peer], dst_ref=incoming.at[sl], send_sem=a2a_send.at[0], recv_sem=a2a_recv.at[pos // 2],
            device_id={"space": peer}, device_id_type=MESH,
        )

    def slots(first, count, group):
        part = incoming.at[pl.ds(first, count)]
        return pltpu.make_async_remote_copy(
            src_ref=outg.at[pl.ds(first, count)], dst_ref=part, send_sem=a2a_send.at[0], recv_sem=a2a_recv.at[group],
            device_id={"space": (me + 1) % SPACE}, device_id_type=MESH,
        )

    pl.semaphore_wait(near_sem.at[1], 1)
    for pos in (1, 0, 2, 3, 4, 5, 6, 7):
        for j in range(8):
            if SHIFTS[pos] or j:
                a2a_copy(pos, j).start()
    incoming[0] = outg[me]

    table[256:256 + NODES, :] = dot(nodes, tgtw[...]).astype(bf16)
    lax.fori_loop(EARLY, BUILDS, build, 0)
    ready("edgew", "edgeb", "e0", "e1")
    ebias = edgeb[...].astype(f32)

    def own(e, _):
        rows = pl.ds(pl.multiple_of(e * ECH, ECH), ECH)
        acc1[rows, :] = dot(edge[rows, :], edgew[...]) + dot(onehot[rows, 0:512], table[...]) + ebias
        return 0

    lax.fori_loop(0, EDGES // ECH, own, 0)

    ready("selfw", "nodeb", "readn", "readw", "msgw", "inw", "outw", "gain")
    self_part = dot(nodes, selfw[...]) + nodeb[...].astype(f32)
    ids = lax.broadcasted_iota(i32, (NODES, LON), 0)
    for r in range(BAND):
        w = jnp.zeros((NODES, LON), f32)
        for corner in range(3):
            w = w + jnp.where(ids == readn[corner, r:r + 1, :], readw[corner, r:r + 1, :], 0.0)
        rwt[:, 0:LON] = w
        rwt[:, LON:LONP] = jnp.zeros((NODES, LONP - LON), f32)
        for tile in range(LONP // 128):
            rmat[r, tile * 128:(tile + 1) * 128, :] = rwt[:, tile * 128:(tile + 1) * 128].T.astype(bf16)
    rmat_copy = pltpu.make_async_copy(rmat, rmat_h, rmat_sem.at[0])
    rmat_copy.start()

    def group_table(g):
        left = incoming[16 * g:16 * g + 8].reshape(256, COLS)
        right = incoming[16 * g + 8:16 * g + 16].reshape(256, COLS)
        return jnp.concatenate([left, right], axis=1)

    def arrive(g):
        first = 1 if g == 0 else 0
        slots(16 * g + first, 16 - first, g).wait_recv()

    for g in range(3):
        arrive(g)
        tg = group_table(g)

        def remote_part(e, _, g=g, tg=tg):
            rows = pl.ds(pl.multiple_of(e * ECH, ECH), ECH)
            d = dot(onehot[rows, 512 + 256 * g:768 + 256 * g], tg)
            if g == 0:
                base = acc1[rows, :]
                acc2[rows, :] = d + jnp.concatenate([base, base], axis=1)
            else:
                acc2[rows, :] = acc2[rows, :] + d
            return 0

        lax.fori_loop(0, EDGES // ECH, remote_part, 0)
    arrive(3)
    tg = group_table(3)

    def finish(e, pooled):
        rows = pl.ds(pl.multiple_of(e * ECH, ECH), ECH)
        d = dot(onehot[rows, 1280:1536], tg) + acc2[rows, :]
        pre = jnp.where(half_b[rows, :].astype(f32) > 0.5, d[:, COLS:], d[:, :COLS])
        return pooled + dot(pool_p[:, rows], silu(pre).astype(bf16))

    pooled = lax.fori_loop(0, EDGES // ECH, finish, jnp.zeros((NODES, COLS), f32))
    pool4[ch] = pooled.astype(bf16)
    g_pool = gather_start(pool4, 1)
    for c in g_pool:
        c.wait_recv()
    message = dot(gathered(pool4), msgw[...]).astype(bf16)
    hid4[ch] = silu(self_part + dot(message, inw[...])).astype(bf16)
    g_hid = gather_start(hid4, 2)
    for c in g_hid:
        c.wait_recv()
    update = dot(gathered(hid4), outw[...])
    mean = jnp.mean(update, axis=1, keepdims=True)
    centred = update - mean
    var = jnp.mean(jnp.square(centred), axis=1, keepdims=True)
    upd[...] = gain[...] * centred * lax.rsqrt(var + norm_eps)
    own_cols = pl.ds(pl.multiple_of(ch * COLS, COLS), COLS)
    result = (mine.astype(f32) + upd[:, own_cols]).astype(bf16)
    node_out[...] = result

    halo[0].wait_send()
    halo[1].wait_send()
    for c in g_nodes + g_pool + g_hid:
        c.wait_send()
    slots(0, SPACE - 1, 0).wait_send()
    rmat_copy.wait()


def read_back(grid_h, rmat_h, node_h, node_o, grid_o, x, rmat, node, out, sem):
    ch = lax.axis_index("chan")
    own_cols = pl.ds(pl.multiple_of(ch * COLS, COLS), COLS)
    node_in = pltpu.make_async_copy(node_h, node, sem.at[6])
    node_in.start()
    bands = []
    for r in range(BAND):
        bands.append((
            pltpu.make_async_copy(grid_h.at[r, :, own_cols], x.at[r], sem.at[r]),
            pltpu.make_async_copy(rmat_h.at[r, 0:LON], rmat.at[r], sem.at[8 + r]),
        ))
        for c in bands[-1]:
            c.start()
    done = [pltpu.make_async_copy(node_h, node_o, sem.at[7])]
    done[0].start()
    node_in.wait()
    result = node[...]
    for r in range(BAND):
        for c in bands[r]:
            c.wait()
        for m in range(LON // MCH):
            rows = pl.ds(m * MCH, MCH)
            out[r, rows, :] = (x[r, rows, :].astype(f32) + dot(rmat[r, rows, :], result)).astype(bf16)
        c = pltpu.make_async_copy(out.at[r], grid_o.at[r], sem.at[3 + r])
        c.start()
        done.append(c)
    for c in done:
        c.wait()


def shards(*args):
    (grid_state, fold_columns, mesh_state, edge_state, conv_weight, conv_bias, source_weight, target_weight,
     edge_weight, edge_bias, message_weight, self_weight, inbox_weight, node_bias, output_weight, output_gain,
     cell_node, cell_weight, edge_source, edge_target, edge_count, send_rows, read_node, read_weight) = args
    anyspace = pl.BlockSpec(memory_space=pl.ANY)
    vmem = pl.BlockSpec(memory_space=pltpu.VMEM)
    V = pltpu.VMEM
    in_specs = [anyspace] * 24
    in_specs[20] = pl.BlockSpec(memory_space=pltpu.SMEM)
    result, rmat = pl.pallas_call(
        kernel,
        out_shape=(
            jax.ShapeDtypeStruct((NODES, COLS), bf16),
            jax.ShapeDtypeStruct((BAND, LONP, NODES), bf16),
        ),
        in_specs=in_specs,
        out_specs=(vmem, anyspace),
        scratch_shapes=[
            V((BAND, LON, FEAT), bf16), V((LON,), i32), V((NODES, COLS), bf16), V((EDGES, FEAT), bf16),
            V((3, FEAT, 3 * COLS), bf16), V((1, COLS), bf16), V((FEAT, COLS), bf16), V((FEAT, COLS), bf16),
            V((FEAT, COLS), bf16), V((1, COLS), bf16),
            V((FEAT, FEAT), bf16), V((FEAT, COLS), bf16), V((FEAT, COLS), bf16), V((1, COLS), bf16),
            V((FEAT, FEAT), bf16), V((1, FEAT), f32), V((BAND, LON), i32), V((BAND, LON), f32),
            V((40, 128), i32), V((40, 128), i32), V((CAP, SPACE), i32), V((3, BAND, LON), i32), V((3, BAND, LON), f32),
            V((LON + 16, 3 * COLS), f32), V((2, LON, COLS), f32), V((2, LON, COLS), bf16), V((2, LON, COLS), bf16),
            V((BAND, LON, COLS), bf16), V((BAND, NODES, LON), bf16), V((SPACE * CAP, 256), bf16),
            V((SPACE, CAP, COLS), bf16), V((512, COLS), bf16),
            V((CHAN, NODES, COLS), bf16), V((CHAN, NODES, COLS), bf16), V((CHAN, NODES, COLS), bf16),
            V((EDGES, 1536), bf16), V((EDGES, 128), bf16), V((NODES, EDGES), bf16),
            V((EDGES, COLS), f32), V((EDGES, 2 * COLS), f32), V((SPACE, CAP, COLS), bf16),
            V((3, 40, 128), i32), V((NODES, LONP), f32), V((BAND, LONP, NODES), bf16), V((NODES, FEAT), f32),
            V((LON, LON), bf16),
            pltpu.SemaphoreType.DMA((40,)), pltpu.SemaphoreType.DMA((2,)), pltpu.SemaphoreType.DMA((2,)),
            pltpu.SemaphoreType.DMA((3, CHAN)), pltpu.SemaphoreType.DMA((3, CHAN)),
            pltpu.SemaphoreType.DMA((1,)), pltpu.SemaphoreType.DMA((4,)), pltpu.SemaphoreType.DMA((1,)),
            pltpu.SemaphoreType.REGULAR((2,)),
        ],
        compiler_params=pltpu.CompilerParams(
            collective_id=0, has_side_effects=True, vmem_limit_bytes=60 * 1024 * 1024
        ),
    )(
        grid_state, fold_columns, mesh_state, edge_state, conv_weight, conv_bias.reshape(1, COLS),
        source_weight, target_weight, edge_weight, edge_bias.reshape(1, COLS), message_weight, self_weight,
        inbox_weight, node_bias.reshape(1, COLS), output_weight, output_gain.reshape(1, FEAT), cell_node, cell_weight,
        edge_source.reshape(40, 128), edge_target.reshape(40, 128), edge_count, send_rows.transpose(0, 2, 1), read_node, read_weight,
    )
    return pl.pallas_call(
        read_back,
        out_shape=(
            jax.ShapeDtypeStruct((NODES, COLS), bf16),
            jax.ShapeDtypeStruct((BAND, LON, COLS), bf16),
        ),
        in_specs=[anyspace, anyspace, anyspace],
        out_specs=(anyspace, anyspace),
        scratch_shapes=[
            V((BAND, LON, COLS), bf16), V((BAND, LON, NODES), bf16), V((NODES, COLS), bf16),
            V((BAND, LON, COLS), bf16), pltpu.SemaphoreType.DMA((11,)),
        ],
    )(grid_state, rmat, result)


def solution(mesh):
    in_specs = (
        P("space", None, None), P(), P("space", "chan"), P("space", None), P(None, None, None, "chan"), P("chan"),
        P(None, "chan"), P(None, "chan"), P(None, "chan"), P("chan"), P(), P(None, "chan"), P(None, "chan"), P("chan"),
        P(), P(), P("space", None), P("space", None), P("space"), P("space"), P("space"), P("space", None, None),
        P(None, "space", None), P(None, "space", None),
    )
    out_specs = (P("space", "chan"), P("space", None, "chan"))
    return jax.shard_map(shards, mesh=mesh, in_specs=in_specs, out_specs=out_specs, check_vma=False)
```

```python
import jax
import jax.numpy as jnp
from jax import lax
from jax.experimental import pallas as pl
from jax.experimental.pallas import tpu as pltpu
from jax.sharding import PartitionSpec as P

f32 = jnp.float32
bf16 = jnp.bfloat16
i32 = jnp.int32
norm_eps = 1e-05
MESH = pl.DeviceIdType.MESH

SPACE, CHAN = 64, 4
NY, NZ, NX = 2, 8, 4
FEAT, COLS = 512, 128
BAND, LON = 3, 720
NODES = 160
EDGES = 5120
CAP = 32
MCH = 240
LONP = 768
SHIFTS = (0, 4, 3, 5, 2, 6, 1, 7)
ECH = 1280
UNROLL = 4
EARLY = 4


def dot(a, b):
    return jnp.dot(a, b, preferred_element_type=f32)


def silu(v):
    return 0.5 * v * (1.0 + jnp.tanh(0.5 * v))


def kernel(
    grid_h, fold_h, mesh_h, edge_h, convw_h, convb_h, srcw_h, tgtw_h, edgew_h, edgeb_h,
    msgw_h, selfw_h, inw_h, nodeb_h, outw_h, gain_h, celln_h, cellw_h, esrc_h, etgt_h,
    ecount, send_h, readn_h, readw_h,
    node_out, rmat_h,
    x, fold, mesh_v, edge, wcat, convb, srcw, tgtw, edgew, edgeb,
    msgw, selfw, nodeb, outw, gain, celln, cellw, esrc, etgt, sendr, readn, readw,
    z, cpart, halo_out, halo_in, act, inc_a, sel_o, outg, table, nodes4, pool4, self4, inw4, both,
    onehot, half_b, pool_p, acc1, acc2, incoming, ridx, rwt, rmat, upd, srcc,
    load_sem, halo_send, halo_recv, gat_send, gat_recv, a2a_send, a2a_recv, rmat_sem, near_sem,
):
    me = lax.axis_index("space")
    ch = lax.axis_index("chan")
    my, mz, mx = me // 32, (me // 4) % 8, me % 4

    loads = {}

    def load(name, src, dst):
        k = len(loads)
        c = pltpu.make_async_copy(src, dst, load_sem.at[k])
        c.start()
        loads[name] = c

    def ready(*names):
        for name in names:
            loads[name].wait()

    def load_w(a):
        for b in range(3):
            load(("w", a, b), convw_h.at[a, b], wcat.at[a, :, b * COLS:(b + 1) * COLS])

    load("x0", grid_h.at[0], x.at[0])
    load_w(2)
    load("x2", grid_h.at[2], x.at[2])
    load_w(0)
    load("x1", grid_h.at[1], x.at[1])
    load_w(1)

    barrier = pltpu.get_barrier_semaphore()

    def hail(sem, **where):
        pl.semaphore_signal(sem, inc=1, device_id=where, device_id_type=MESH)

    y_at = [((my + d) % NY) * 32 for d in range(NY)]
    z_at = [((mz + d) % NZ) * 4 for d in range(NZ)]
    x_at = [(mx + d) % NX for d in range(NX)]

    def at(dy, dz, dx):
        return y_at[dy] + z_at[dz] + x_at[dx]

    hail(barrier, space=(me + 1) % SPACE)
    hail(barrier, space=(me + SPACE - 1) % SPACE)
    for d in range(1, CHAN):
        hail(barrier, chan=(ch + d) % CHAN)
    hail(barrier, space=at(1, 0, 0))
    for d in range(1, NX):
        hail(barrier, space=at(0, 0, d))
    for d in range(1, NZ):
        hail(barrier, space=at(0, d, 0))
    for name, s, d in (
        ("convb", convb_h, convb), ("celln", celln_h, celln), ("cellw", cellw_h, cellw),
        ("inw", inw_h, inw4.at[ch]),
        ("sendr", send_h.at[0], sendr), ("fold", fold_h, fold), ("mesh", mesh_h, mesh_v), ("srcw", srcw_h, srcw),
    ):
        load(name, s, d)

    sibling = ch + 1 - 2 * (ch % 2)
    group = ((ch + 2) % CHAN, (sibling + 2) % CHAN, sibling)

    def gather_start(buf, stage):
        out = []
        for k, peer in enumerate(group):
            c = pltpu.make_async_remote_copy(
                src_ref=buf.at[ch], dst_ref=buf.at[ch], send_sem=gat_send.at[stage, k], recv_sem=gat_recv.at[stage, k],
                device_id={"chan": peer}, device_id_type=MESH,
            )
            c.start()
            out.append(c)
        return out

    def gathered(buf):
        return jnp.concatenate([buf[c] for c in range(CHAN)], axis=1)

    def conv_z(terms):
        for m in range(LON // MCH):
            rows = pl.ds(m * MCH, MCH)
            acc = None
            for xr, a in terms:
                d = dot(xr[rows, :], wcat[a])
                acc = d if acc is None else acc + d
            z[pl.ds(8 + m * MCH, MCH), :] = acc
        z[7:8, 0:COLS] = z[LON + 7:LON + 8, 0:COLS]
        z[LON + 8:LON + 9, 2 * COLS:3 * COLS] = z[8:9, 2 * COLS:3 * COLS]

    def shifted(m):
        o = m * MCH
        return (
            z[pl.ds(o + 7, MCH), 0:COLS]
            + z[pl.ds(o + 8, MCH), COLS:2 * COLS]
            + z[pl.ds(o + 9, MCH), 2 * COLS:3 * COLS]
        )

    chunks = range(LON // MCH)

    ready("x0", ("w", 2, 0), ("w", 2, 1), ("w", 2, 2))
    conv_z([(x.at[0], 2)])
    for m in chunks:
        halo_out[0, pl.ds(m * MCH, MCH), :] = shifted(m).astype(bf16)
    pl.semaphore_wait(barrier, 2 + CHAN - 1 + NY - 1 + NX - 1 + NZ - 1)
    for d in range(1, NX):
        hail(near_sem.at[0], space=at(0, 0, d))

    def halo_copy(k):
        peer = (me + SPACE - 1) % SPACE if k == 0 else (me + 1) % SPACE
        return pltpu.make_async_remote_copy(
            src_ref=halo_out.at[k], dst_ref=halo_in.at[k], send_sem=halo_send.at[k], recv_sem=halo_recv.at[k],
            device_id={"space": peer}, device_id_type=MESH,
        )

    halo = [halo_copy(0), halo_copy(1)]
    halo[0].start()
    ready("x2", ("w", 0, 0), ("w", 0, 1), ("w", 0, 2))
    conv_z([(x.at[2], 0)])
    for m in chunks:
        halo_out[1, pl.ds(m * MCH, MCH), :] = shifted(m).astype(bf16)
    halo[1].start()
    ready("inw")
    g_inw = gather_start(inw4, 1)
    pl.semaphore_wait(near_sem.at[0], NX - 1)
    hail(near_sem.at[1], space=at(1, 0, 0))

    ready("x1", ("w", 1, 0), ("w", 1, 1), ("w", 1, 2), "convb", "celln", "cellw")
    for name, s, d in (
        ("esrc", esrc_h, esrc), ("etgt", etgt_h, etgt), ("tgtw", tgtw_h, tgtw),
        ("edgew", edgew_h, edgew), ("edgeb", edgeb_h, edgeb),
        ("e0", edge_h.at[0:2560], edge.at[0:2560]), ("e1", edge_h.at[2560:5120], edge.at[2560:5120]),
        ("selfw", selfw_h, selfw), ("msgw", msgw_h, msgw), ("nodeb", nodeb_h, nodeb),
        ("outw", outw_h, outw), ("gain", gain_h, gain), ("readn", readn_h, readn), ("readw", readw_h, readw),
    ):
        load(name, s, d)
    bias = convb[...].astype(f32)
    for r, terms in (
        (0, [(x.at[0], 1), (x.at[1], 2)]),
        (2, [(x.at[1], 0), (x.at[2], 1)]),
        (1, [(x.at[0], 0), (x.at[1], 1), (x.at[2], 2)]),
    ):
        conv_z(terms)
        for m in chunks:
            v = shifted(m) + bias
            rows = pl.ds(m * MCH, MCH)
            if r == 1:
                act[1, rows, :] = silu(v).astype(bf16)
            else:
                cpart[r // 2, rows, :] = v

    ready("fold")

    @pl.when(me == SPACE - 1)
    def _():
        def body(t, _):
            rows = pl.ds(pl.multiple_of(t * 16, 16), 16)
            ids = lax.broadcasted_iota(i32, (16, LON), 0) + t * 16
            pick = jnp.where(ids == fold[...].reshape(1, LON), 1.0, 0.0).astype(bf16)
            srcc[rows, :] = pick
            return 0

        lax.fori_loop(0, LON // 16, body, 0)
        xf = lax.dot_general(srcc[...], x[2], (((0,), (0,)), ((), ())), preferred_element_type=f32)
        upd_x = xf.astype(bf16)
        onehot[0:LON, 0:FEAT] = upd_x
        conv_z([(onehot.at[0:LON, 0:FEAT], 2)])
        for m in chunks:
            rows = pl.ds(m * MCH, MCH)
            cpart[1, rows, :] = cpart[1, rows, :] + shifted(m)

    for r in range(BAND):
        ids = lax.broadcasted_iota(i32, (NODES, LON), 0)
        inc_a[r] = jnp.where(ids == celln[r:r + 1, :], cellw[r:r + 1, :], 0.0).astype(bf16)

    ready("sendr")
    send_t = sendr[...].astype(f32)
    lane256 = lax.broadcasted_iota(i32, (CAP, 256), 1).astype(f32)
    for p in range(SPACE):
        sel_o[p * CAP:(p + 1) * CAP, :] = jnp.where(send_t[:, p:p + 1] == lane256, 1.0, 0.0).astype(bf16)

    halo[0].wait_recv()
    halo[1].wait_recv()
    south_ok = jnp.where(me > 0, 1.0, 0.0)
    north_ok = jnp.where(me < SPACE - 1, 1.0, 0.0)
    for m in chunks:
        rows = pl.ds(m * MCH, MCH)
        act[0, rows, :] = silu(cpart[0, rows, :] + halo_in[1, rows, :].astype(f32) * south_ok).astype(bf16)
        act[2, rows, :] = silu(cpart[1, rows, :] + halo_in[0, rows, :].astype(f32) * north_ok).astype(bf16)
    ready("mesh")
    agg = dot(inc_a[0], act[0]) + dot(inc_a[1], act[1]) + dot(inc_a[2], act[2])
    mine = (mesh_v[...].astype(f32) + agg).astype(bf16)

    nodes4[ch] = mine
    g_nodes = gather_start(nodes4, 0)
    ready("srcw", "tgtw")
    table[...] = jnp.zeros_like(table)

    ready("esrc", "etgt")
    s = esrc[...]
    u = s - NODES
    q = lax.shift_right_logical(u, 5) & 63
    k = u & 31
    dz = (mz - (lax.shift_right_logical(q, 2) & 7)) & 7
    dy = (my - lax.shift_right_logical(q, 5)) & 1
    dx = (mx - (q & 3)) & 3
    t = jnp.zeros_like(s)
    for pos, shift in enumerate(SHIFTS):
        t = jnp.where(dz == shift, pos, t)
    remote = 256 + lax.shift_right_logical(t, 1) * 256 + (dy * 4 + dx) * CAP + k
    col = jnp.where(u < 0, s, remote)
    halfbit = jnp.where(u < 0, 0, t & 1)
    slot = lax.broadcasted_iota(i32, s.shape, 0) * 128 + lax.broadcasted_iota(i32, s.shape, 1)
    live_t = jnp.where(slot < ecount[0], etgt[...], -1)
    srcc2 = col + 2048 * halfbit
    ridx[0] = srcc2
    ridx[1] = etgt[...]
    ridx[2] = live_t

    lane_f = lax.broadcasted_iota(i32, (128, 128), 1).astype(f32)

    def column(which, e):
        row = ridx[which, pl.ds(e, 1), :].astype(f32)
        return jnp.broadcast_to(row, (128, 128)).T

    def build_one(e):
        rows = pl.ds(pl.multiple_of(e * 128, 128), 128)
        c = column(0, e)
        hb = jnp.where(c >= 2048.0, 1.0, 0.0)
        half_b[rows, :] = hb.astype(bf16)
        c = c - 2048.0 * hb
        hi = jnp.floor(c * (1.0 / 128.0))
        lo = c - 128.0 * hi
        m = jnp.where(lo == lane_f, hi, -1.0).astype(bf16)
        one = jnp.ones((128, 128), bf16)
        zero = jnp.zeros((128, 128), bf16)
        for tile in range(10):
            to = tile if tile < 2 else tile + 2
            onehot[rows, to * 128:(to + 1) * 128] = jnp.where(m == jnp.asarray(tile, bf16), one, zero)
        c = column(1, e)
        for tile in range(2):
            onehot[rows, (2 + tile) * 128:(3 + tile) * 128] = jnp.where(
                c == lane_f + 128.0 * tile, 1.0, 0.0
            ).astype(bf16)
        ids = lax.broadcasted_iota(i32, (NODES, 128), 0)
        pool_p[:, rows] = jnp.where(ids == ridx[2, pl.ds(e, 1), :], 1.0, 0.0).astype(bf16)

    def build(b, _):
        for k in range(UNROLL):
            build_one(b * UNROLL + k)
        return 0

    BUILDS = EDGES // 128 // UNROLL
    lax.fori_loop(0, EARLY, build, 0)
    for c in g_nodes:
        c.wait_recv()
    nodes = gathered(nodes4)
    sent = dot(nodes, srcw[...]).astype(bf16)
    table[0:NODES, :] = sent
    for b in range(SPACE * CAP // 256):
        picked = dot(sel_o[b * 256:(b + 1) * 256, :], table[0:256, :]).astype(bf16)
        outg[b * 8:(b + 1) * 8] = picked.reshape(8, CAP, COLS)

    def a2a_copy(pos, j):
        peer = y_at[j // 4] + z_at[SHIFTS[pos]] + x_at[j % 4]
        sl = pos * 8 + j
        return pltpu.make_async_remote_copy(
            src_ref=outg.at[peer], dst_ref=incoming.at[sl], send_sem=a2a_send.at[0], recv_sem=a2a_recv.at[pos // 2],
            device_id={"space": peer}, device_id_type=MESH,
        )

    def slots(first, count, group):
        part = incoming.at[pl.ds(first, count)]
        return pltpu.make_async_remote_copy(
            src_ref=outg.at[pl.ds(first, count)], dst_ref=part, send_sem=a2a_send.at[0], recv_sem=a2a_recv.at[group],
            device_id={"space": (me + 1) % SPACE}, device_id_type=MESH,
        )

    pl.semaphore_wait(near_sem.at[1], 1)
    for pos in (1, 0, 2, 3, 4, 5, 6, 7):
        for j in range(8):
            if SHIFTS[pos] or j:
                a2a_copy(pos, j).start()
    incoming[0] = outg[me]

    ready("selfw", "nodeb")
    self4[ch] = (dot(nodes, selfw[...]) + nodeb[...].astype(f32)).astype(bf16)
    g_self = gather_start(self4, 2)
    table[256:256 + NODES, :] = dot(nodes, tgtw[...]).astype(bf16)
    lax.fori_loop(EARLY, BUILDS, build, 0)
    ready("edgew", "edgeb", "e0", "e1")
    ebias = edgeb[...].astype(f32)

    def own(e, _):
        rows = pl.ds(pl.multiple_of(e * ECH, ECH), ECH)
        acc1[rows, :] = dot(edge[rows, :], edgew[...]) + dot(onehot[rows, 0:512], table[...]) + ebias
        return 0

    lax.fori_loop(0, EDGES // ECH, own, 0)

    ready("readn", "readw", "msgw", "outw", "gain")
    for c in g_inw + g_self:
        c.wait_recv()
    both[...] = dot(msgw[...], gathered(inw4)).astype(bf16)
    ids = lax.broadcasted_iota(i32, (NODES, LON), 0)
    for r in range(BAND):
        w = jnp.zeros((NODES, LON), f32)
        for corner in range(3):
            w = w + jnp.where(ids == readn[corner, r:r + 1, :], readw[corner, r:r + 1, :], 0.0)
        rwt[:, 0:LON] = w
        rwt[:, LON:LONP] = jnp.zeros((NODES, LONP - LON), f32)
        for tile in range(LONP // 128):
            rmat[r, tile * 128:(tile + 1) * 128, :] = rwt[:, tile * 128:(tile + 1) * 128].T.astype(bf16)
    rmat_copy = pltpu.make_async_copy(rmat, rmat_h, rmat_sem.at[0])
    rmat_copy.start()

    def group_table(g):
        left = incoming[16 * g:16 * g + 8].reshape(256, COLS)
        right = incoming[16 * g + 8:16 * g + 16].reshape(256, COLS)
        return jnp.concatenate([left, right], axis=1)

    def arrive(g):
        first = 1 if g == 0 else 0
        slots(16 * g + first, 16 - first, g).wait_recv()

    for g in range(3):
        arrive(g)
        tg = group_table(g)

        def remote_part(e, _, g=g, tg=tg):
            rows = pl.ds(pl.multiple_of(e * ECH, ECH), ECH)
            d = dot(onehot[rows, 512 + 256 * g:768 + 256 * g], tg)
            if g == 0:
                base = acc1[rows, :]
                acc2[rows, :] = d + jnp.concatenate([base, base], axis=1)
            else:
                acc2[rows, :] = acc2[rows, :] + d
            return 0

        lax.fori_loop(0, EDGES // ECH, remote_part, 0)
    arrive(3)
    tg = group_table(3)

    def finish(e, pooled):
        rows = pl.ds(pl.multiple_of(e * ECH, ECH), ECH)
        d = dot(onehot[rows, 1280:1536], tg) + acc2[rows, :]
        pre = jnp.where(half_b[rows, :].astype(f32) > 0.5, d[:, COLS:], d[:, :COLS])
        return pooled + dot(pool_p[:, rows], silu(pre).astype(bf16))

    pooled = lax.fori_loop(0, EDGES // ECH, finish, jnp.zeros((NODES, COLS), f32))
    pool4[ch] = pooled.astype(bf16)
    g_pool = gather_start(pool4, 3)
    for c in g_pool:
        c.wait_recv()
    hidden = silu(gathered(self4).astype(f32) + dot(gathered(pool4), both[...])).astype(bf16)
    update = dot(hidden, outw[...])
    mean = jnp.mean(update, axis=1, keepdims=True)
    centred = update - mean
    var = jnp.mean(jnp.square(centred), axis=1, keepdims=True)
    upd[...] = gain[...] * centred * lax.rsqrt(var + norm_eps)
    own_cols = pl.ds(pl.multiple_of(ch * COLS, COLS), COLS)
    result = (mine.astype(f32) + upd[:, own_cols]).astype(bf16)
    node_out[...] = result

    halo[0].wait_send()
    halo[1].wait_send()
    for c in g_nodes + g_inw + g_self + g_pool:
        c.wait_send()
    slots(0, SPACE - 1, 0).wait_send()
    rmat_copy.wait()


def read_back(grid_h, rmat_h, node_h, node_o, grid_o, x, rmat, node, out, sem):
    ch = lax.axis_index("chan")
    own_cols = pl.ds(pl.multiple_of(ch * COLS, COLS), COLS)
    node_in = pltpu.make_async_copy(node_h, node, sem.at[6])
    node_in.start()
    bands = []
    for r in range(BAND):
        bands.append((
            pltpu.make_async_copy(grid_h.at[r, :, own_cols], x.at[r], sem.at[r]),
            pltpu.make_async_copy(rmat_h.at[r, 0:LON], rmat.at[r], sem.at[8 + r]),
        ))
        for c in bands[-1]:
            c.start()
    done = [pltpu.make_async_copy(node_h, node_o, sem.at[7])]
    done[0].start()
    node_in.wait()
    result = node[...]
    for r in range(BAND):
        for c in bands[r]:
            c.wait()
        for m in range(LON // MCH):
            rows = pl.ds(m * MCH, MCH)
            out[r, rows, :] = (x[r, rows, :].astype(f32) + dot(rmat[r, rows, :], result)).astype(bf16)
        c = pltpu.make_async_copy(out.at[r], grid_o.at[r], sem.at[3 + r])
        c.start()
        done.append(c)
    for c in done:
        c.wait()


def shards(*args):
    (grid_state, fold_columns, mesh_state, edge_state, conv_weight, conv_bias, source_weight, target_weight,
     edge_weight, edge_bias, message_weight, self_weight, inbox_weight, node_bias, output_weight, output_gain,
     cell_node, cell_weight, edge_source, edge_target, edge_count, send_rows, read_node, read_weight) = args
    anyspace = pl.BlockSpec(memory_space=pl.ANY)
    vmem = pl.BlockSpec(memory_space=pltpu.VMEM)
    V = pltpu.VMEM
    in_specs = [anyspace] * 24
    in_specs[20] = pl.BlockSpec(memory_space=pltpu.SMEM)
    result, rmat = pl.pallas_call(
        kernel,
        out_shape=(
            jax.ShapeDtypeStruct((NODES, COLS), bf16),
            jax.ShapeDtypeStruct((BAND, LONP, NODES), bf16),
        ),
        in_specs=in_specs,
        out_specs=(vmem, anyspace),
        scratch_shapes=[
            V((BAND, LON, FEAT), bf16), V((LON,), i32), V((NODES, COLS), bf16), V((EDGES, FEAT), bf16),
            V((3, FEAT, 3 * COLS), bf16), V((1, COLS), bf16), V((FEAT, COLS), bf16), V((FEAT, COLS), bf16),
            V((FEAT, COLS), bf16), V((1, COLS), bf16),
            V((FEAT, FEAT), bf16), V((FEAT, COLS), bf16), V((1, COLS), bf16),
            V((FEAT, FEAT), bf16), V((1, FEAT), f32), V((BAND, LON), i32), V((BAND, LON), f32),
            V((40, 128), i32), V((40, 128), i32), V((CAP, SPACE), i32), V((3, BAND, LON), i32), V((3, BAND, LON), f32),
            V((LON + 16, 3 * COLS), f32), V((2, LON, COLS), f32), V((2, LON, COLS), bf16), V((2, LON, COLS), bf16),
            V((BAND, LON, COLS), bf16), V((BAND, NODES, LON), bf16), V((SPACE * CAP, 256), bf16),
            V((SPACE, CAP, COLS), bf16), V((512, COLS), bf16),
            V((CHAN, NODES, COLS), bf16), V((CHAN, NODES, COLS), bf16), V((CHAN, NODES, COLS), bf16),
            V((CHAN, FEAT, COLS), bf16), V((FEAT, FEAT), bf16),
            V((EDGES, 1536), bf16), V((EDGES, 128), bf16), V((NODES, EDGES), bf16),
            V((EDGES, COLS), f32), V((EDGES, 2 * COLS), f32), V((SPACE, CAP, COLS), bf16),
            V((3, 40, 128), i32), V((NODES, LONP), f32), V((BAND, LONP, NODES), bf16), V((NODES, FEAT), f32),
            V((LON, LON), bf16),
            pltpu.SemaphoreType.DMA((40,)), pltpu.SemaphoreType.DMA((2,)), pltpu.SemaphoreType.DMA((2,)),
            pltpu.SemaphoreType.DMA((4, 3)), pltpu.SemaphoreType.DMA((4, 3)),
            pltpu.SemaphoreType.DMA((1,)), pltpu.SemaphoreType.DMA((4,)), pltpu.SemaphoreType.DMA((1,)),
            pltpu.SemaphoreType.REGULAR((2,)),
        ],
        compiler_params=pltpu.CompilerParams(
            collective_id=0, has_side_effects=True, vmem_limit_bytes=60 * 1024 * 1024
        ),
    )(
        grid_state, fold_columns, mesh_state, edge_state, conv_weight, conv_bias.reshape(1, COLS),
        source_weight, target_weight, edge_weight, edge_bias.reshape(1, COLS), message_weight, self_weight,
        inbox_weight, node_bias.reshape(1, COLS), output_weight, output_gain.reshape(1, FEAT), cell_node, cell_weight,
        edge_source.reshape(40, 128), edge_target.reshape(40, 128), edge_count, send_rows.transpose(0, 2, 1), read_node, read_weight,
    )
    return pl.pallas_call(
        read_back,
        out_shape=(
            jax.ShapeDtypeStruct((NODES, COLS), bf16),
            jax.ShapeDtypeStruct((BAND, LON, COLS), bf16),
        ),
        in_specs=[anyspace, anyspace, anyspace],
        out_specs=(anyspace, anyspace),
        scratch_shapes=[
            V((BAND, LON, COLS), bf16), V((BAND, LON, NODES), bf16), V((NODES, COLS), bf16),
            V((BAND, LON, COLS), bf16), pltpu.SemaphoreType.DMA((11,)),
        ],
    )(grid_state, rmat, result)


def solution(mesh):
    in_specs = (
        P("space", None, None), P(), P("space", "chan"), P("space", None), P(None, None, None, "chan"), P("chan"),
        P(None, "chan"), P(None, "chan"), P(None, "chan"), P("chan"), P(), P(None, "chan"), P(None, "chan"), P("chan"),
        P(), P(), P("space", None), P("space", None), P("space"), P("space"), P("space"), P("space", None, None),
        P(None, "space", None), P(None, "space", None),
    )
    out_specs = (P("space", "chan"), P("space", None, "chan"))
    return jax.shard_map(shards, mesh=mesh, in_specs=in_specs, out_specs=out_specs, check_vma=False)
```

```python
import jax
import jax.numpy as jnp
from jax import lax
from jax.experimental import pallas as pl
from jax.experimental.pallas import tpu as pltpu
from jax.sharding import PartitionSpec as P

f32 = jnp.float32
bf16 = jnp.bfloat16
i32 = jnp.int32
norm_eps = 1e-05
MESH = pl.DeviceIdType.MESH

SPACE, CHAN = 64, 4
NY, NZ, NX = 2, 8, 4
FEAT, COLS = 512, 128
BAND, LON = 3, 720
NODES = 160
EDGES = 5120
CAP = 32
MCH = 240
LONP = 768
SHIFTS = (0, 4, 3, 5, 2, 6, 1, 7)
ECH = 2560
UNROLL = 8
EARLY = 2


def dot(a, b):
    return jnp.dot(a, b, preferred_element_type=f32)


def silu(v):
    return 0.5 * v * (1.0 + jnp.tanh(0.5 * v))


def kernel(
    grid_h, fold_h, mesh_h, edge_h, convw_h, convb_h, srcw_h, tgtw_h, edgew_h, edgeb_h,
    msgw_h, selfw_h, inw_h, nodeb_h, outw_h, gain_h, celln_h, cellw_h, esrc_h, etgt_h,
    ecount, send_h, readn_h, readw_h,
    node_out, rmat_h,
    x, fold, mesh_v, edge, wcat, convb, srcw, tgtw, edgew, edgeb,
    msgw, selfw, nodeb, outw, gain, celln, cellw, esrc, etgt, sendr, readn, readw,
    z, cpart, halo_out, halo_in, act, inc_a, sel_o, outg, table, nodes4, pool4, self4, inw4, both,
    onehot, half_b, pool_p, acc1, acc2, incoming, ridx, rwt, rmat, upd, srcc,
    load_sem, halo_send, halo_recv, gat_send, gat_recv, a2a_send, a2a_recv, rmat_sem, near_sem,
):
    me = lax.axis_index("space")
    ch = lax.axis_index("chan")
    my, mz, mx = me // 32, (me // 4) % 8, me % 4

    loads = {}

    def load(name, src, dst):
        k = len(loads)
        c = pltpu.make_async_copy(src, dst, load_sem.at[k])
        c.start()
        loads[name] = c

    def ready(*names):
        for name in names:
            loads[name].wait()

    def load_w(a):
        for b in range(3):
            load(("w", a, b), convw_h.at[a, b], wcat.at[a, :, b * COLS:(b + 1) * COLS])

    load("x0", grid_h.at[0], x.at[0])
    load_w(2)
    load("x2", grid_h.at[2], x.at[2])
    load_w(0)
    load("x1", grid_h.at[1], x.at[1])
    load_w(1)

    barrier = pltpu.get_barrier_semaphore()

    def hail(sem, **where):
        pl.semaphore_signal(sem, inc=1, device_id=where, device_id_type=MESH)

    y_at = [((my + d) % NY) * 32 for d in range(NY)]
    z_at = [((mz + d) % NZ) * 4 for d in range(NZ)]
    x_at = [(mx + d) % NX for d in range(NX)]

    def at(dy, dz, dx):
        return y_at[dy] + z_at[dz] + x_at[dx]

    hail(barrier, space=(me + 1) % SPACE)
    hail(barrier, space=(me + SPACE - 1) % SPACE)
    for d in range(1, CHAN):
        hail(barrier, chan=(ch + d) % CHAN)
    hail(barrier, space=at(1, 0, 0))
    for d in range(1, NX):
        hail(barrier, space=at(0, 0, d))
    for d in range(1, NZ):
        hail(barrier, space=at(0, d, 0))
    for name, s, d in (
        ("convb", convb_h, convb), ("celln", celln_h, celln), ("cellw", cellw_h, cellw),
        ("inw", inw_h, inw4.at[ch]),
        ("sendr", send_h.at[0], sendr), ("fold", fold_h, fold), ("mesh", mesh_h, mesh_v), ("srcw", srcw_h, srcw),
    ):
        load(name, s, d)

    sibling = ch + 1 - 2 * (ch % 2)
    group = ((ch + 2) % CHAN, (sibling + 2) % CHAN, sibling)

    def gather_start(buf, stage):
        out = []
        for k, peer in enumerate(group):
            c = pltpu.make_async_remote_copy(
                src_ref=buf.at[ch], dst_ref=buf.at[ch], send_sem=gat_send.at[stage, k], recv_sem=gat_recv.at[stage, k],
                device_id={"chan": peer}, device_id_type=MESH,
            )
            c.start()
            out.append(c)
        return out

    def gathered(buf):
        return jnp.concatenate([buf[c] for c in range(CHAN)], axis=1)

    def conv_z(terms):
        for m in range(LON // MCH):
            rows = pl.ds(m * MCH, MCH)
            acc = None
            for xr, a in terms:
                d = dot(xr[rows, :], wcat[a])
                acc = d if acc is None else acc + d
            z[pl.ds(8 + m * MCH, MCH), :] = acc
        z[7:8, 0:COLS] = z[LON + 7:LON + 8, 0:COLS]
        z[LON + 8:LON + 9, 2 * COLS:3 * COLS] = z[8:9, 2 * COLS:3 * COLS]

    def shifted(m):
        o = m * MCH
        return (
            z[pl.ds(o + 7, MCH), 0:COLS]
            + z[pl.ds(o + 8, MCH), COLS:2 * COLS]
            + z[pl.ds(o + 9, MCH), 2 * COLS:3 * COLS]
        )

    chunks = range(LON // MCH)

    ready("x0", ("w", 2, 0), ("w", 2, 1), ("w", 2, 2))
    conv_z([(x.at[0], 2)])
    for m in chunks:
        halo_out[0, pl.ds(m * MCH, MCH), :] = shifted(m).astype(bf16)
    pl.semaphore_wait(barrier, 2 + CHAN - 1 + NY - 1 + NX - 1 + NZ - 1)
    for d in range(1, NX):
        hail(near_sem.at[0], space=at(0, 0, d))

    def halo_copy(k):
        peer = (me + SPACE - 1) % SPACE if k == 0 else (me + 1) % SPACE
        return pltpu.make_async_remote_copy(
            src_ref=halo_out.at[k], dst_ref=halo_in.at[k], send_sem=halo_send.at[k], recv_sem=halo_recv.at[k],
            device_id={"space": peer}, device_id_type=MESH,
        )

    halo = [halo_copy(0), halo_copy(1)]
    halo[0].start()
    ready("x2", ("w", 0, 0), ("w", 0, 1), ("w", 0, 2))
    conv_z([(x.at[2], 0)])
    for m in chunks:
        halo_out[1, pl.ds(m * MCH, MCH), :] = shifted(m).astype(bf16)
    halo[1].start()
    ready("inw")
    g_inw = gather_start(inw4, 1)
    pl.semaphore_wait(near_sem.at[0], NX - 1)
    hail(near_sem.at[1], space=at(1, 0, 0))

    ready("x1", ("w", 1, 0), ("w", 1, 1), ("w", 1, 2), "convb", "celln", "cellw")
    for name, s, d in (
        ("esrc", esrc_h, esrc), ("etgt", etgt_h, etgt), ("tgtw", tgtw_h, tgtw),
        ("edgew", edgew_h, edgew), ("edgeb", edgeb_h, edgeb),
        ("e0", edge_h.at[0:2560], edge.at[0:2560]), ("e1", edge_h.at[2560:5120], edge.at[2560:5120]),
        ("selfw", selfw_h, selfw), ("msgw", msgw_h, msgw), ("nodeb", nodeb_h, nodeb),
        ("outw", outw_h, outw), ("gain", gain_h, gain), ("readn", readn_h, readn), ("readw", readw_h, readw),
    ):
        load(name, s, d)
    bias = convb[...].astype(f32)
    for r, terms in (
        (0, [(x.at[0], 1), (x.at[1], 2)]),
        (2, [(x.at[1], 0), (x.at[2], 1)]),
        (1, [(x.at[0], 0), (x.at[1], 1), (x.at[2], 2)]),
    ):
        conv_z(terms)
        for m in chunks:
            v = shifted(m) + bias
            rows = pl.ds(m * MCH, MCH)
            if r == 1:
                act[1, rows, :] = silu(v).astype(bf16)
            else:
                cpart[r // 2, rows, :] = v

    ready("fold")

    @pl.when(me == SPACE - 1)
    def _():
        def body(t, _):
            rows = pl.ds(pl.multiple_of(t * 16, 16), 16)
            ids = lax.broadcasted_iota(i32, (16, LON), 0) + t * 16
            pick = jnp.where(ids == fold[...].reshape(1, LON), 1.0, 0.0).astype(bf16)
            srcc[rows, :] = pick
            return 0

        lax.fori_loop(0, LON // 16, body, 0)
        xf = lax.dot_general(srcc[...], x[2], (((0,), (0,)), ((), ())), preferred_element_type=f32)
        upd_x = xf.astype(bf16)
        onehot[0:LON, 0:FEAT] = upd_x
        conv_z([(onehot.at[0:LON, 0:FEAT], 2)])
        for m in chunks:
            rows = pl.ds(m * MCH, MCH)
            cpart[1, rows, :] = cpart[1, rows, :] + shifted(m)

    for r in range(BAND):
        ids = lax.broadcasted_iota(i32, (NODES, LON), 0)
        inc_a[r] = jnp.where(ids == celln[r:r + 1, :], cellw[r:r + 1, :], 0.0).astype(bf16)

    ready("sendr")
    send_t = sendr[...].astype(f32)
    lane256 = lax.broadcasted_iota(i32, (CAP, 256), 1).astype(f32)
    for p in range(SPACE):
        sel_o[p * CAP:(p + 1) * CAP, :] = jnp.where(send_t[:, p:p + 1] == lane256, 1.0, 0.0).astype(bf16)

    halo[0].wait_recv()
    halo[1].wait_recv()
    south_ok = jnp.where(me > 0, 1.0, 0.0)
    north_ok = jnp.where(me < SPACE - 1, 1.0, 0.0)
    for m in chunks:
        rows = pl.ds(m * MCH, MCH)
        act[0, rows, :] = silu(cpart[0, rows, :] + halo_in[1, rows, :].astype(f32) * south_ok).astype(bf16)
        act[2, rows, :] = silu(cpart[1, rows, :] + halo_in[0, rows, :].astype(f32) * north_ok).astype(bf16)
    ready("mesh")
    agg = dot(inc_a[0], act[0]) + dot(inc_a[1], act[1]) + dot(inc_a[2], act[2])
    mine = (mesh_v[...].astype(f32) + agg).astype(bf16)

    nodes4[ch] = mine
    g_nodes = gather_start(nodes4, 0)
    ready("srcw", "tgtw")
    table[...] = jnp.zeros_like(table)

    ready("esrc", "etgt")
    s = esrc[...]
    u = s - NODES
    q = lax.shift_right_logical(u, 5) & 63
    k = u & 31
    dz = (mz - (lax.shift_right_logical(q, 2) & 7)) & 7
    dy = (my - lax.shift_right_logical(q, 5)) & 1
    dx = (mx - (q & 3)) & 3
    t = jnp.zeros_like(s)
    for pos, shift in enumerate(SHIFTS):
        t = jnp.where(dz == shift, pos, t)
    remote = 256 + lax.shift_right_logical(t, 1) * 256 + (dy * 4 + dx) * CAP + k
    col = jnp.where(u < 0, s, remote)
    halfbit = jnp.where(u < 0, 0, t & 1)
    slot = lax.broadcasted_iota(i32, s.shape, 0) * 128 + lax.broadcasted_iota(i32, s.shape, 1)
    live_t = jnp.where(slot < ecount[0], etgt[...], -1)
    srcc2 = col + 2048 * halfbit
    ridx[0] = srcc2
    ridx[1] = etgt[...]
    ridx[2] = live_t

    lane_f = lax.broadcasted_iota(i32, (128, 128), 1).astype(f32)

    def column(which, e):
        row = ridx[which, pl.ds(e, 1), :].astype(f32)
        return jnp.broadcast_to(row, (128, 128)).T

    def build_one(e):
        rows = pl.ds(pl.multiple_of(e * 128, 128), 128)
        c = column(0, e)
        hb = jnp.where(c >= 2048.0, 1.0, 0.0)
        half_b[rows, :] = hb.astype(bf16)
        c = c - 2048.0 * hb
        hi = jnp.floor(c * (1.0 / 128.0))
        lo = c - 128.0 * hi
        m = jnp.where(lo == lane_f, hi, -1.0).astype(bf16)
        one = jnp.ones((128, 128), bf16)
        zero = jnp.zeros((128, 128), bf16)
        for tile in range(10):
            to = tile if tile < 2 else tile + 2
            onehot[rows, to * 128:(to + 1) * 128] = jnp.where(m == jnp.asarray(tile, bf16), one, zero)
        c = column(1, e)
        for tile in range(2):
            onehot[rows, (2 + tile) * 128:(3 + tile) * 128] = jnp.where(
                c == lane_f + 128.0 * tile, 1.0, 0.0
            ).astype(bf16)
        ids = lax.broadcasted_iota(i32, (NODES, 128), 0)
        pool_p[:, rows] = jnp.where(ids == ridx[2, pl.ds(e, 1), :], 1.0, 0.0).astype(bf16)

    def build(b, _):
        for k in range(UNROLL):
            build_one(b * UNROLL + k)
        return 0

    BUILDS = EDGES // 128 // UNROLL
    lax.fori_loop(0, EARLY, build, 0)
    for c in g_nodes:
        c.wait_recv()
    nodes = gathered(nodes4)
    sent = dot(nodes, srcw[...]).astype(bf16)
    table[0:NODES, :] = sent
    for b in range(SPACE * CAP // 256):
        picked = dot(sel_o[b * 256:(b + 1) * 256, :], table[0:256, :]).astype(bf16)
        outg[b * 8:(b + 1) * 8] = picked.reshape(8, CAP, COLS)

    def a2a_copy(pos, j):
        peer = y_at[j // 4] + z_at[SHIFTS[pos]] + x_at[j % 4]
        sl = pos * 8 + j
        return pltpu.make_async_remote_copy(
            src_ref=outg.at[peer], dst_ref=incoming.at[sl], send_sem=a2a_send.at[0], recv_sem=a2a_recv.at[pos // 2],
            device_id={"space": peer}, device_id_type=MESH,
        )

    def slots(first, count, group):
        part = incoming.at[pl.ds(first, count)]
        return pltpu.make_async_remote_copy(
            src_ref=outg.at[pl.ds(first, count)], dst_ref=part, send_sem=a2a_send.at[0], recv_sem=a2a_recv.at[group],
            device_id={"space": (me + 1) % SPACE}, device_id_type=MESH,
        )

    pl.semaphore_wait(near_sem.at[1], 1)
    for pos in (1, 0, 2, 3, 4, 5, 6, 7):
        for j in range(8):
            if SHIFTS[pos] or j:
                a2a_copy(pos, j).start()
    incoming[0] = outg[me]

    ready("selfw", "nodeb")
    self4[ch] = (dot(nodes, selfw[...]) + nodeb[...].astype(f32)).astype(bf16)
    g_self = gather_start(self4, 2)
    table[256:256 + NODES, :] = dot(nodes, tgtw[...]).astype(bf16)
    lax.fori_loop(EARLY, BUILDS, build, 0)
    ready("edgew", "edgeb", "e0", "e1")
    ebias = edgeb[...].astype(f32)

    def own(e, _):
        rows = pl.ds(pl.multiple_of(e * ECH, ECH), ECH)
        acc1[rows, :] = dot(edge[rows, :], edgew[...]) + dot(onehot[rows, 0:512], table[...]) + ebias
        return 0

    lax.fori_loop(0, EDGES // ECH, own, 0)

    ready("readn", "readw", "msgw", "outw", "gain")
    for c in g_inw + g_self:
        c.wait_recv()
    both[...] = dot(msgw[...], gathered(inw4)).astype(bf16)
    ids = lax.broadcasted_iota(i32, (NODES, LON), 0)
    for r in range(BAND):
        w = jnp.zeros((NODES, LON), f32)
        for corner in range(3):
            w = w + jnp.where(ids == readn[corner, r:r + 1, :], readw[corner, r:r + 1, :], 0.0)
        rwt[:, 0:LON] = w
        rwt[:, LON:LONP] = jnp.zeros((NODES, LONP - LON), f32)
        for tile in range(LONP // 128):
            rmat[r, tile * 128:(tile + 1) * 128, :] = rwt[:, tile * 128:(tile + 1) * 128].T.astype(bf16)
    rmat_copy = pltpu.make_async_copy(rmat, rmat_h, rmat_sem.at[0])
    rmat_copy.start()

    def group_table(g):
        left = incoming[16 * g:16 * g + 8].reshape(256, COLS)
        right = incoming[16 * g + 8:16 * g + 16].reshape(256, COLS)
        return jnp.concatenate([left, right], axis=1)

    def arrive(g):
        first = 1 if g == 0 else 0
        slots(16 * g + first, 16 - first, g).wait_recv()

    for g in range(3):
        arrive(g)
        tg = group_table(g)

        def remote_part(e, _, g=g, tg=tg):
            rows = pl.ds(pl.multiple_of(e * ECH, ECH), ECH)
            d = dot(onehot[rows, 512 + 256 * g:768 + 256 * g], tg)
            if g == 0:
                base = acc1[rows, :]
                acc2[rows, :] = d + jnp.concatenate([base, base], axis=1)
            else:
                acc2[rows, :] = acc2[rows, :] + d
            return 0

        lax.fori_loop(0, EDGES // ECH, remote_part, 0)
    arrive(3)
    tg = group_table(3)

    def finish(e, pooled):
        rows = pl.ds(pl.multiple_of(e * ECH, ECH), ECH)
        d = dot(onehot[rows, 1280:1536], tg) + acc2[rows, :]
        pre = jnp.where(half_b[rows, :].astype(f32) > 0.5, d[:, COLS:], d[:, :COLS])
        return pooled + dot(pool_p[:, rows], silu(pre).astype(bf16))

    pooled = lax.fori_loop(0, EDGES // ECH, finish, jnp.zeros((NODES, COLS), f32))
    pool4[ch] = pooled.astype(bf16)
    g_pool = gather_start(pool4, 3)
    for c in g_pool:
        c.wait_recv()
    hidden = silu(gathered(self4).astype(f32) + dot(gathered(pool4), both[...])).astype(bf16)
    update = dot(hidden, outw[...])
    mean = jnp.mean(update, axis=1, keepdims=True)
    centred = update - mean
    var = jnp.mean(jnp.square(centred), axis=1, keepdims=True)
    upd[...] = gain[...] * centred * lax.rsqrt(var + norm_eps)
    own_cols = pl.ds(pl.multiple_of(ch * COLS, COLS), COLS)
    result = (mine.astype(f32) + upd[:, own_cols]).astype(bf16)
    node_out[...] = result

    halo[0].wait_send()
    halo[1].wait_send()
    for c in g_nodes + g_inw + g_self + g_pool:
        c.wait_send()
    slots(0, SPACE - 1, 0).wait_send()
    rmat_copy.wait()


def read_back(grid_h, rmat_h, node_h, node_o, grid_o, x, rmat, node, out, sem):
    ch = lax.axis_index("chan")
    own_cols = pl.ds(pl.multiple_of(ch * COLS, COLS), COLS)
    node_in = pltpu.make_async_copy(node_h, node, sem.at[6])
    node_in.start()
    bands = []
    for r in range(BAND):
        bands.append((
            pltpu.make_async_copy(grid_h.at[r, :, own_cols], x.at[r], sem.at[r]),
            pltpu.make_async_copy(rmat_h.at[r, 0:LON], rmat.at[r], sem.at[8 + r]),
        ))
        for c in bands[-1]:
            c.start()
    done = [pltpu.make_async_copy(node_h, node_o, sem.at[7])]
    done[0].start()
    node_in.wait()
    result = node[...]
    for r in range(BAND):
        for c in bands[r]:
            c.wait()
        for m in range(LON // MCH):
            rows = pl.ds(m * MCH, MCH)
            out[r, rows, :] = (x[r, rows, :].astype(f32) + dot(rmat[r, rows, :], result)).astype(bf16)
        c = pltpu.make_async_copy(out.at[r], grid_o.at[r], sem.at[3 + r])
        c.start()
        done.append(c)
    for c in done:
        c.wait()


def shards(*args):
    (grid_state, fold_columns, mesh_state, edge_state, conv_weight, conv_bias, source_weight, target_weight,
     edge_weight, edge_bias, message_weight, self_weight, inbox_weight, node_bias, output_weight, output_gain,
     cell_node, cell_weight, edge_source, edge_target, edge_count, send_rows, read_node, read_weight) = args
    anyspace = pl.BlockSpec(memory_space=pl.ANY)
    vmem = pl.BlockSpec(memory_space=pltpu.VMEM)
    V = pltpu.VMEM
    in_specs = [anyspace] * 24
    in_specs[20] = pl.BlockSpec(memory_space=pltpu.SMEM)
    result, rmat = pl.pallas_call(
        kernel,
        out_shape=(
            jax.ShapeDtypeStruct((NODES, COLS), bf16),
            jax.ShapeDtypeStruct((BAND, LONP, NODES), bf16),
        ),
        in_specs=in_specs,
        out_specs=(vmem, anyspace),
        scratch_shapes=[
            V((BAND, LON, FEAT), bf16), V((LON,), i32), V((NODES, COLS), bf16), V((EDGES, FEAT), bf16),
            V((3, FEAT, 3 * COLS), bf16), V((1, COLS), bf16), V((FEAT, COLS), bf16), V((FEAT, COLS), bf16),
            V((FEAT, COLS), bf16), V((1, COLS), bf16),
            V((FEAT, FEAT), bf16), V((FEAT, COLS), bf16), V((1, COLS), bf16),
            V((FEAT, FEAT), bf16), V((1, FEAT), f32), V((BAND, LON), i32), V((BAND, LON), f32),
            V((40, 128), i32), V((40, 128), i32), V((CAP, SPACE), i32), V((3, BAND, LON), i32), V((3, BAND, LON), f32),
            V((LON + 16, 3 * COLS), f32), V((2, LON, COLS), f32), V((2, LON, COLS), bf16), V((2, LON, COLS), bf16),
            V((BAND, LON, COLS), bf16), V((BAND, NODES, LON), bf16), V((SPACE * CAP, 256), bf16),
            V((SPACE, CAP, COLS), bf16), V((512, COLS), bf16),
            V((CHAN, NODES, COLS), bf16), V((CHAN, NODES, COLS), bf16), V((CHAN, NODES, COLS), bf16),
            V((CHAN, FEAT, COLS), bf16), V((FEAT, FEAT), bf16),
            V((EDGES, 1536), bf16), V((EDGES, 128), bf16), V((NODES, EDGES), bf16),
            V((EDGES, COLS), f32), V((EDGES, 2 * COLS), f32), V((SPACE, CAP, COLS), bf16),
            V((3, 40, 128), i32), V((NODES, LONP), f32), V((BAND, LONP, NODES), bf16), V((NODES, FEAT), f32),
            V((LON, LON), bf16),
            pltpu.SemaphoreType.DMA((40,)), pltpu.SemaphoreType.DMA((2,)), pltpu.SemaphoreType.DMA((2,)),
            pltpu.SemaphoreType.DMA((4, 3)), pltpu.SemaphoreType.DMA((4, 3)),
            pltpu.SemaphoreType.DMA((1,)), pltpu.SemaphoreType.DMA((4,)), pltpu.SemaphoreType.DMA((1,)),
            pltpu.SemaphoreType.REGULAR((2,)),
        ],
        compiler_params=pltpu.CompilerParams(
            collective_id=0, has_side_effects=True, vmem_limit_bytes=60 * 1024 * 1024
        ),
    )(
        grid_state, fold_columns, mesh_state, edge_state, conv_weight, conv_bias.reshape(1, COLS),
        source_weight, target_weight, edge_weight, edge_bias.reshape(1, COLS), message_weight, self_weight,
        inbox_weight, node_bias.reshape(1, COLS), output_weight, output_gain.reshape(1, FEAT), cell_node, cell_weight,
        edge_source.reshape(40, 128), edge_target.reshape(40, 128), edge_count, send_rows.transpose(0, 2, 1), read_node, read_weight,
    )
    return pl.pallas_call(
        read_back,
        out_shape=(
            jax.ShapeDtypeStruct((NODES, COLS), bf16),
            jax.ShapeDtypeStruct((BAND, LON, COLS), bf16),
        ),
        in_specs=[anyspace, anyspace, anyspace],
        out_specs=(anyspace, anyspace),
        scratch_shapes=[
            V((BAND, LON, COLS), bf16), V((BAND, LON, NODES), bf16), V((NODES, COLS), bf16),
            V((BAND, LON, COLS), bf16), pltpu.SemaphoreType.DMA((11,)),
        ],
    )(grid_state, rmat, result)


def solution(mesh):
    in_specs = (
        P("space", None, None), P(), P("space", "chan"), P("space", None), P(None, None, None, "chan"), P("chan"),
        P(None, "chan"), P(None, "chan"), P(None, "chan"), P("chan"), P(), P(None, "chan"), P(None, "chan"), P("chan"),
        P(), P(), P("space", None), P("space", None), P("space"), P("space"), P("space"), P("space", None, None),
        P(None, "space", None), P(None, "space", None),
    )
    out_specs = (P("space", "chan"), P("space", None, "chan"))
    return jax.shard_map(shards, mesh=mesh, in_specs=in_specs, out_specs=out_specs, check_vma=False)
```

```python
import jax
import jax.numpy as jnp
from jax import lax
from jax.experimental import pallas as pl
from jax.experimental.pallas import tpu as pltpu
from jax.sharding import PartitionSpec as P

f32 = jnp.float32
bf16 = jnp.bfloat16
i32 = jnp.int32
norm_eps = 1e-05
MESH = pl.DeviceIdType.MESH

SPACE, CHAN = 64, 4
NY, NZ, NX = 2, 8, 4
FEAT, COLS = 512, 128
BAND, LON = 3, 720
NODES = 160
EDGES = 5120
CAP = 32
MCH = 240
LONP = 768
SHIFTS = (0, 4, 3, 5, 2, 6, 1, 7)
ECH = 2560
UNROLL = 20
EARLY = 1


def dot(a, b):
    return jnp.dot(a, b, preferred_element_type=f32)


def silu(v):
    return 0.5 * v * (1.0 + jnp.tanh(0.5 * v))


def kernel(
    grid_h, fold_h, mesh_h, edge_h, convw_h, convb_h, srcw_h, tgtw_h, edgew_h, edgeb_h,
    msgw_h, selfw_h, inw_h, nodeb_h, outw_h, gain_h, celln_h, cellw_h, esrc_h, etgt_h,
    ecount, send_h, readn_h, readw_h,
    node_out, rmat_h,
    x, fold, mesh_v, edge, wcat, convb, srcw, tgtw, edgew, edgeb,
    msgw, selfw, nodeb, outw, gain, celln, cellw, esrc, etgt, sendr, readn, readw,
    z, cpart, halo_out, halo_in, act, inc_a, sel_o, outg, table, nodes4, pool4, self4, inw4, both,
    onehot, half_b, pool_p, acc1, acc2, incoming, ridx, rwt, rmat, upd, srcc,
    load_sem, halo_send, halo_recv, gat_send, gat_recv, a2a_send, a2a_recv, rmat_sem, near_sem,
):
    me = lax.axis_index("space")
    ch = lax.axis_index("chan")
    my, mz, mx = me // 32, (me // 4) % 8, me % 4

    loads = {}

    def load(name, src, dst):
        k = len(loads)
        c = pltpu.make_async_copy(src, dst, load_sem.at[k])
        c.start()
        loads[name] = c

    def ready(*names):
        for name in names:
            loads[name].wait()

    def load_w(a):
        for b in range(3):
            load(("w", a, b), convw_h.at[a, b], wcat.at[a, :, b * COLS:(b + 1) * COLS])

    load("x0", grid_h.at[0], x.at[0])
    load_w(2)
    load("x2", grid_h.at[2], x.at[2])
    load_w(0)
    load("x1", grid_h.at[1], x.at[1])
    load_w(1)

    barrier = pltpu.get_barrier_semaphore()

    def hail(sem, **where):
        pl.semaphore_signal(sem, inc=1, device_id=where, device_id_type=MESH)

    y_at = [((my + d) % NY) * 32 for d in range(NY)]
    z_at = [((mz + d) % NZ) * 4 for d in range(NZ)]
    x_at = [(mx + d) % NX for d in range(NX)]

    def at(dy, dz, dx):
        return y_at[dy] + z_at[dz] + x_at[dx]

    hail(barrier, space=(me + 1) % SPACE)
    hail(barrier, space=(me + SPACE - 1) % SPACE)
    for d in range(1, CHAN):
        hail(barrier, chan=(ch + d) % CHAN)
    hail(barrier, space=at(1, 0, 0))
    for d in range(1, NX):
        hail(barrier, space=at(0, 0, d))
    for d in range(1, NZ):
        hail(barrier, space=at(0, d, 0))
    for name, s, d in (
        ("convb", convb_h, convb), ("celln", celln_h, celln), ("cellw", cellw_h, cellw),
        ("inw", inw_h, inw4.at[ch]),
        ("sendr", send_h.at[0], sendr), ("fold", fold_h, fold), ("mesh", mesh_h, mesh_v), ("srcw", srcw_h, srcw),
    ):
        load(name, s, d)

    sibling = ch + 1 - 2 * (ch % 2)
    group = ((ch + 2) % CHAN, (sibling + 2) % CHAN, sibling)

    def gather_start(buf, stage):
        out = []
        for k, peer in enumerate(group):
            c = pltpu.make_async_remote_copy(
                src_ref=buf.at[ch], dst_ref=buf.at[ch], send_sem=gat_send.at[stage, k], recv_sem=gat_recv.at[stage, k],
                device_id={"chan": peer}, device_id_type=MESH,
            )
            c.start()
            out.append(c)
        return out

    def gathered(buf):
        return jnp.concatenate([buf[c] for c in range(CHAN)], axis=1)

    def conv_z(terms):
        for m in range(LON // MCH):
            rows = pl.ds(m * MCH, MCH)
            acc = None
            for xr, a in terms:
                d = dot(xr[rows, :], wcat[a])
                acc = d if acc is None else acc + d
            z[pl.ds(8 + m * MCH, MCH), :] = acc
        z[7:8, 0:COLS] = z[LON + 7:LON + 8, 0:COLS]
        z[LON + 8:LON + 9, 2 * COLS:3 * COLS] = z[8:9, 2 * COLS:3 * COLS]

    def shifted(m):
        o = m * MCH
        return (
            z[pl.ds(o + 7, MCH), 0:COLS]
            + z[pl.ds(o + 8, MCH), COLS:2 * COLS]
            + z[pl.ds(o + 9, MCH), 2 * COLS:3 * COLS]
        )

    chunks = range(LON // MCH)

    ready("x0", ("w", 2, 0), ("w", 2, 1), ("w", 2, 2))
    conv_z([(x.at[0], 2)])
    for m in chunks:
        halo_out[0, pl.ds(m * MCH, MCH), :] = shifted(m).astype(bf16)
    pl.semaphore_wait(barrier, 2 + CHAN - 1 + NY - 1 + NX - 1 + NZ - 1)
    for d in range(1, NX):
        hail(near_sem.at[0], space=at(0, 0, d))

    def halo_copy(k):
        peer = (me + SPACE - 1) % SPACE if k == 0 else (me + 1) % SPACE
        return pltpu.make_async_remote_copy(
            src_ref=halo_out.at[k], dst_ref=halo_in.at[k], send_sem=halo_send.at[k], recv_sem=halo_recv.at[k],
            device_id={"space": peer}, device_id_type=MESH,
        )

    halo = [halo_copy(0), halo_copy(1)]
    halo[0].start()
    ready("x2", ("w", 0, 0), ("w", 0, 1), ("w", 0, 2))
    conv_z([(x.at[2], 0)])
    for m in chunks:
        halo_out[1, pl.ds(m * MCH, MCH), :] = shifted(m).astype(bf16)
    halo[1].start()
    ready("inw")
    g_inw = gather_start(inw4, 1)
    pl.semaphore_wait(near_sem.at[0], NX - 1)
    hail(near_sem.at[1], space=at(1, 0, 0))

    ready("x1", ("w", 1, 0), ("w", 1, 1), ("w", 1, 2), "convb", "celln", "cellw")
    for name, s, d in (
        ("esrc", esrc_h, esrc), ("etgt", etgt_h, etgt), ("tgtw", tgtw_h, tgtw),
        ("edgew", edgew_h, edgew), ("edgeb", edgeb_h, edgeb),
        ("e0", edge_h.at[0:2560], edge.at[0:2560]), ("e1", edge_h.at[2560:5120], edge.at[2560:5120]),
        ("selfw", selfw_h, selfw), ("msgw", msgw_h, msgw), ("nodeb", nodeb_h, nodeb),
        ("outw", outw_h, outw), ("gain", gain_h, gain), ("readn", readn_h, readn), ("readw", readw_h, readw),
    ):
        load(name, s, d)
    bias = convb[...].astype(f32)
    for r, terms in (
        (0, [(x.at[0], 1), (x.at[1], 2)]),
        (2, [(x.at[1], 0), (x.at[2], 1)]),
        (1, [(x.at[0], 0), (x.at[1], 1), (x.at[2], 2)]),
    ):
        conv_z(terms)
        for m in chunks:
            v = shifted(m) + bias
            rows = pl.ds(m * MCH, MCH)
            if r == 1:
                act[1, rows, :] = silu(v).astype(bf16)
            else:
                cpart[r // 2, rows, :] = v

    ready("fold")

    @pl.when(me == SPACE - 1)
    def _():
        def body(t, _):
            rows = pl.ds(pl.multiple_of(t * 16, 16), 16)
            ids = lax.broadcasted_iota(i32, (16, LON), 0) + t * 16
            pick = jnp.where(ids == fold[...].reshape(1, LON), 1.0, 0.0).astype(bf16)
            srcc[rows, :] = pick
            return 0

        lax.fori_loop(0, LON // 16, body, 0)
        xf = lax.dot_general(srcc[...], x[2], (((0,), (0,)), ((), ())), preferred_element_type=f32)
        upd_x = xf.astype(bf16)
        onehot[0:LON, 0:FEAT] = upd_x
        conv_z([(onehot.at[0:LON, 0:FEAT], 2)])
        for m in chunks:
            rows = pl.ds(m * MCH, MCH)
            cpart[1, rows, :] = cpart[1, rows, :] + shifted(m)

    for r in range(BAND):
        ids = lax.broadcasted_iota(i32, (NODES, LON), 0)
        inc_a[r] = jnp.where(ids == celln[r:r + 1, :], cellw[r:r + 1, :], 0.0).astype(bf16)

    halo[0].wait_recv()
    halo[1].wait_recv()
    south_ok = jnp.where(me > 0, 1.0, 0.0)
    north_ok = jnp.where(me < SPACE - 1, 1.0, 0.0)
    for m in chunks:
        rows = pl.ds(m * MCH, MCH)
        act[0, rows, :] = silu(cpart[0, rows, :] + halo_in[1, rows, :].astype(f32) * south_ok).astype(bf16)
        act[2, rows, :] = silu(cpart[1, rows, :] + halo_in[0, rows, :].astype(f32) * north_ok).astype(bf16)
    ready("mesh")
    agg = dot(inc_a[0], act[0]) + dot(inc_a[1], act[1]) + dot(inc_a[2], act[2])
    mine = (mesh_v[...].astype(f32) + agg).astype(bf16)

    nodes4[ch] = mine
    g_nodes = gather_start(nodes4, 0)
    ready("srcw", "tgtw")
    table[...] = jnp.zeros_like(table)

    ready("sendr")
    send_t = sendr[...].astype(f32)
    lane256 = lax.broadcasted_iota(i32, (CAP, 256), 1).astype(f32)
    for p in range(SPACE):
        sel_o[p * CAP:(p + 1) * CAP, :] = jnp.where(send_t[:, p:p + 1] == lane256, 1.0, 0.0).astype(bf16)

    ready("esrc", "etgt")
    s = esrc[...]
    u = s - NODES
    q = lax.shift_right_logical(u, 5) & 63
    k = u & 31
    dz = (mz - (lax.shift_right_logical(q, 2) & 7)) & 7
    dy = (my - lax.shift_right_logical(q, 5)) & 1
    dx = (mx - (q & 3)) & 3
    t = jnp.zeros_like(s)
    for pos, shift in enumerate(SHIFTS):
        t = jnp.where(dz == shift, pos, t)
    remote = 256 + lax.shift_right_logical(t, 1) * 256 + (dy * 4 + dx) * CAP + k
    col = jnp.where(u < 0, s, remote)
    halfbit = jnp.where(u < 0, 0, t & 1)
    slot = lax.broadcasted_iota(i32, s.shape, 0) * 128 + lax.broadcasted_iota(i32, s.shape, 1)
    live_t = jnp.where(slot < ecount[0], etgt[...], -1)
    srcc2 = col + 2048 * halfbit
    ridx[0] = srcc2
    ridx[1] = etgt[...]
    ridx[2] = live_t

    lane_f = lax.broadcasted_iota(i32, (128, 128), 1).astype(f32)

    def column(which, e):
        row = ridx[which, pl.ds(e, 1), :].astype(f32)
        return jnp.broadcast_to(row, (128, 128)).T

    def build_one(e):
        rows = pl.ds(pl.multiple_of(e * 128, 128), 128)
        c = column(0, e)
        hb = jnp.where(c >= 2048.0, 1.0, 0.0)
        half_b[rows, :] = hb.astype(bf16)
        c = c - 2048.0 * hb
        hi = jnp.floor(c * (1.0 / 128.0))
        lo = c - 128.0 * hi
        m = jnp.where(lo == lane_f, hi, -1.0).astype(bf16)
        one = jnp.ones((128, 128), bf16)
        zero = jnp.zeros((128, 128), bf16)
        for tile in range(10):
            to = tile if tile < 2 else tile + 2
            onehot[rows, to * 128:(to + 1) * 128] = jnp.where(m == jnp.asarray(tile, bf16), one, zero)
        c = column(1, e)
        for tile in range(2):
            onehot[rows, (2 + tile) * 128:(3 + tile) * 128] = jnp.where(
                c == lane_f + 128.0 * tile, 1.0, 0.0
            ).astype(bf16)
        ids = lax.broadcasted_iota(i32, (NODES, 128), 0)
        pool_p[:, rows] = jnp.where(ids == ridx[2, pl.ds(e, 1), :], 1.0, 0.0).astype(bf16)

    def build(b, _):
        for k in range(UNROLL):
            build_one(b * UNROLL + k)
        return 0

    BUILDS = EDGES // 128 // UNROLL
    lax.fori_loop(0, EARLY, build, 0)
    for c in g_nodes:
        c.wait_recv()
    nodes = gathered(nodes4)
    sent = dot(nodes, srcw[...]).astype(bf16)
    table[0:NODES, :] = sent
    for b in range(SPACE * CAP // 256):
        picked = dot(sel_o[b * 256:(b + 1) * 256, :], table[0:256, :]).astype(bf16)
        outg[b * 8:(b + 1) * 8] = picked.reshape(8, CAP, COLS)

    def a2a_copy(pos, j):
        peer = y_at[j // 4] + z_at[SHIFTS[pos]] + x_at[j % 4]
        sl = pos * 8 + j
        return pltpu.make_async_remote_copy(
            src_ref=outg.at[peer], dst_ref=incoming.at[sl], send_sem=a2a_send.at[0], recv_sem=a2a_recv.at[pos // 2],
            device_id={"space": peer}, device_id_type=MESH,
        )

    def slots(first, count, group):
        part = incoming.at[pl.ds(first, count)]
        return pltpu.make_async_remote_copy(
            src_ref=outg.at[pl.ds(first, count)], dst_ref=part, send_sem=a2a_send.at[0], recv_sem=a2a_recv.at[group],
            device_id={"space": (me + 1) % SPACE}, device_id_type=MESH,
        )

    pl.semaphore_wait(near_sem.at[1], 1)
    for pos in (1, 0, 2, 3, 4, 5, 6, 7):
        for j in range(8):
            if SHIFTS[pos] or j:
                a2a_copy(pos, j).start()
    incoming[0] = outg[me]

    ready("selfw", "nodeb")
    self4[ch] = (dot(nodes, selfw[...]) + nodeb[...].astype(f32)).astype(bf16)
    g_self = gather_start(self4, 2)
    table[256:256 + NODES, :] = dot(nodes, tgtw[...]).astype(bf16)
    lax.fori_loop(EARLY, BUILDS, build, 0)
    ready("edgew", "edgeb", "e0", "e1")
    ebias = edgeb[...].astype(f32)

    def own(e, _):
        rows = pl.ds(pl.multiple_of(e * ECH, ECH), ECH)
        acc1[rows, :] = dot(edge[rows, :], edgew[...]) + dot(onehot[rows, 0:512], table[...]) + ebias
        return 0

    lax.fori_loop(0, EDGES // ECH, own, 0)

    ready("readn", "readw", "msgw", "outw", "gain")
    for c in g_inw + g_self:
        c.wait_recv()
    both[...] = dot(msgw[...], gathered(inw4)).astype(bf16)
    ids = lax.broadcasted_iota(i32, (NODES, LON), 0)
    for r in range(BAND):
        w = jnp.zeros((NODES, LON), f32)
        for corner in range(3):
            w = w + jnp.where(ids == readn[corner, r:r + 1, :], readw[corner, r:r + 1, :], 0.0)
        rwt[:, 0:LON] = w
        rwt[:, LON:LONP] = jnp.zeros((NODES, LONP - LON), f32)
        for tile in range(LONP // 128):
            rmat[r, tile * 128:(tile + 1) * 128, :] = rwt[:, tile * 128:(tile + 1) * 128].T.astype(bf16)
    rmat_copy = pltpu.make_async_copy(rmat, rmat_h, rmat_sem.at[0])
    rmat_copy.start()

    def group_table(g):
        left = incoming[16 * g:16 * g + 8].reshape(256, COLS)
        right = incoming[16 * g + 8:16 * g + 16].reshape(256, COLS)
        return jnp.concatenate([left, right], axis=1)

    def arrive(g):
        first = 1 if g == 0 else 0
        slots(16 * g + first, 16 - first, g).wait_recv()

    for g in range(3):
        arrive(g)
        tg = group_table(g)

        def remote_part(e, _, g=g, tg=tg):
            rows = pl.ds(pl.multiple_of(e * ECH, ECH), ECH)
            d = dot(onehot[rows, 512 + 256 * g:768 + 256 * g], tg)
            if g == 0:
                base = acc1[rows, :]
                acc2[rows, :] = d + jnp.concatenate([base, base], axis=1)
            else:
                acc2[rows, :] = acc2[rows, :] + d
            return 0

        lax.fori_loop(0, EDGES // ECH, remote_part, 0)
    arrive(3)
    tg = group_table(3)

    def finish(e, pooled):
        rows = pl.ds(pl.multiple_of(e * ECH, ECH), ECH)
        d = dot(onehot[rows, 1280:1536], tg) + acc2[rows, :]
        pre = jnp.where(half_b[rows, :].astype(f32) > 0.5, d[:, COLS:], d[:, :COLS])
        return pooled + dot(pool_p[:, rows], silu(pre).astype(bf16))

    pooled = lax.fori_loop(0, EDGES // ECH, finish, jnp.zeros((NODES, COLS), f32))
    pool4[ch] = pooled.astype(bf16)
    g_pool = gather_start(pool4, 3)
    for c in g_pool:
        c.wait_recv()
    hidden = silu(gathered(self4).astype(f32) + dot(gathered(pool4), both[...])).astype(bf16)
    update = dot(hidden, outw[...])
    mean = jnp.mean(update, axis=1, keepdims=True)
    centred = update - mean
    var = jnp.mean(jnp.square(centred), axis=1, keepdims=True)
    upd[...] = gain[...] * centred * lax.rsqrt(var + norm_eps)
    own_cols = pl.ds(pl.multiple_of(ch * COLS, COLS), COLS)
    result = (mine.astype(f32) + upd[:, own_cols]).astype(bf16)
    node_out[...] = result

    halo[0].wait_send()
    halo[1].wait_send()
    for c in g_nodes + g_inw + g_self + g_pool:
        c.wait_send()
    slots(0, SPACE - 1, 0).wait_send()
    rmat_copy.wait()


def read_back(grid_h, rmat_h, node_h, node_o, grid_o, x, rmat, node, out, sem):
    ch = lax.axis_index("chan")
    own_cols = pl.ds(pl.multiple_of(ch * COLS, COLS), COLS)
    node_in = pltpu.make_async_copy(node_h, node, sem.at[6])
    node_in.start()
    bands = []
    for r in range(BAND):
        bands.append((
            pltpu.make_async_copy(grid_h.at[r, :, own_cols], x.at[r], sem.at[r]),
            pltpu.make_async_copy(rmat_h.at[r, 0:LON], rmat.at[r], sem.at[8 + r]),
        ))
        for c in bands[-1]:
            c.start()
    done = [pltpu.make_async_copy(node_h, node_o, sem.at[7])]
    done[0].start()
    node_in.wait()
    result = node[...]
    for r in range(BAND):
        for c in bands[r]:
            c.wait()
        for m in range(LON // MCH):
            rows = pl.ds(m * MCH, MCH)
            out[r, rows, :] = (x[r, rows, :].astype(f32) + dot(rmat[r, rows, :], result)).astype(bf16)
        c = pltpu.make_async_copy(out.at[r], grid_o.at[r], sem.at[3 + r])
        c.start()
        done.append(c)
    for c in done:
        c.wait()


def shards(*args):
    (grid_state, fold_columns, mesh_state, edge_state, conv_weight, conv_bias, source_weight, target_weight,
     edge_weight, edge_bias, message_weight, self_weight, inbox_weight, node_bias, output_weight, output_gain,
     cell_node, cell_weight, edge_source, edge_target, edge_count, send_rows, read_node, read_weight) = args
    anyspace = pl.BlockSpec(memory_space=pl.ANY)
    vmem = pl.BlockSpec(memory_space=pltpu.VMEM)
    V = pltpu.VMEM
    in_specs = [anyspace] * 24
    in_specs[20] = pl.BlockSpec(memory_space=pltpu.SMEM)
    result, rmat = pl.pallas_call(
        kernel,
        out_shape=(
            jax.ShapeDtypeStruct((NODES, COLS), bf16),
            jax.ShapeDtypeStruct((BAND, LONP, NODES), bf16),
        ),
        in_specs=in_specs,
        out_specs=(vmem, anyspace),
        scratch_shapes=[
            V((BAND, LON, FEAT), bf16), V((LON,), i32), V((NODES, COLS), bf16), V((EDGES, FEAT), bf16),
            V((3, FEAT, 3 * COLS), bf16), V((1, COLS), bf16), V((FEAT, COLS), bf16), V((FEAT, COLS), bf16),
            V((FEAT, COLS), bf16), V((1, COLS), bf16),
            V((FEAT, FEAT), bf16), V((FEAT, COLS), bf16), V((1, COLS), bf16),
            V((FEAT, FEAT), bf16), V((1, FEAT), f32), V((BAND, LON), i32), V((BAND, LON), f32),
            V((40, 128), i32), V((40, 128), i32), V((CAP, SPACE), i32), V((3, BAND, LON), i32), V((3, BAND, LON), f32),
            V((LON + 16, 3 * COLS), f32), V((2, LON, COLS), f32), V((2, LON, COLS), bf16), V((2, LON, COLS), bf16),
            V((BAND, LON, COLS), bf16), V((BAND, NODES, LON), bf16), V((SPACE * CAP, 256), bf16),
            V((SPACE, CAP, COLS), bf16), V((512, COLS), bf16),
            V((CHAN, NODES, COLS), bf16), V((CHAN, NODES, COLS), bf16), V((CHAN, NODES, COLS), bf16),
            V((CHAN, FEAT, COLS), bf16), V((FEAT, FEAT), bf16),
            V((EDGES, 1536), bf16), V((EDGES, 128), bf16), V((NODES, EDGES), bf16),
            V((EDGES, COLS), f32), V((EDGES, 2 * COLS), f32), V((SPACE, CAP, COLS), bf16),
            V((3, 40, 128), i32), V((NODES, LONP), f32), V((BAND, LONP, NODES), bf16), V((NODES, FEAT), f32),
            V((LON, LON), bf16),
            pltpu.SemaphoreType.DMA((40,)), pltpu.SemaphoreType.DMA((2,)), pltpu.SemaphoreType.DMA((2,)),
            pltpu.SemaphoreType.DMA((4, 3)), pltpu.SemaphoreType.DMA((4, 3)),
            pltpu.SemaphoreType.DMA((1,)), pltpu.SemaphoreType.DMA((4,)), pltpu.SemaphoreType.DMA((1,)),
            pltpu.SemaphoreType.REGULAR((2,)),
        ],
        compiler_params=pltpu.CompilerParams(
            collective_id=0, has_side_effects=True, vmem_limit_bytes=60 * 1024 * 1024
        ),
    )(
        grid_state, fold_columns, mesh_state, edge_state, conv_weight, conv_bias.reshape(1, COLS),
        source_weight, target_weight, edge_weight, edge_bias.reshape(1, COLS), message_weight, self_weight,
        inbox_weight, node_bias.reshape(1, COLS), output_weight, output_gain.reshape(1, FEAT), cell_node, cell_weight,
        edge_source.reshape(40, 128), edge_target.reshape(40, 128), edge_count, send_rows.transpose(0, 2, 1), read_node, read_weight,
    )
    return pl.pallas_call(
        read_back,
        out_shape=(
            jax.ShapeDtypeStruct((NODES, COLS), bf16),
            jax.ShapeDtypeStruct((BAND, LON, COLS), bf16),
        ),
        in_specs=[anyspace, anyspace, anyspace],
        out_specs=(anyspace, anyspace),
        scratch_shapes=[
            V((BAND, LON, COLS), bf16), V((BAND, LON, NODES), bf16), V((NODES, COLS), bf16),
            V((BAND, LON, COLS), bf16), pltpu.SemaphoreType.DMA((11,)),
        ],
    )(grid_state, rmat, result)


def solution(mesh):
    in_specs = (
        P("space", None, None), P(), P("space", "chan"), P("space", None), P(None, None, None, "chan"), P("chan"),
        P(None, "chan"), P(None, "chan"), P(None, "chan"), P("chan"), P(), P(None, "chan"), P(None, "chan"), P("chan"),
        P(), P(), P("space", None), P("space", None), P("space"), P("space"), P("space"), P("space", None, None),
        P(None, "space", None), P(None, "space", None),
    )
    out_specs = (P("space", "chan"), P("space", None, "chan"))
    return jax.shard_map(shards, mesh=mesh, in_specs=in_specs, out_specs=out_specs, check_vma=False)
```
